256 devices in a mesh: seq: 2 (over core), tp: 4 (over x), req: 32 (over z, y).
Axes of the slice: x: 4, y: 4, z: 8, core: 2. Of those that a mesh axis runs over, the one named last changes fastest.
Arguments:
- cache_pool: bfloat16 [2, 32, 8, 16, 128, 256], P('seq', 'req', 'tp'), may hold values from -6 to 6
- fresh_kv: bfloat16 [32, 8, 256, 256], P('req', 'tp', 'seq'), may hold values from -6.2 to 6.2
- queries: bfloat16 [32, 256, 12288], P('req', 'seq', 'tp'), may hold values from -155 to 155
- stretch_owner: int32 [32, 2], replicated, may hold values from 0 to 48, as said below
- stretch_slot: int32 [32, 2], replicated, may hold values from 0 to 15
- recomp: int32 [32, 2, 1], replicated, may hold values from -1 to 15, as said below
Outputs:
- attended: bfloat16 [32, 256, 12288], P('req', 'seq', 'tp')
- deviation: float32 [32, 256], P('req', 'seq')
The draws below stay inside these ranges and needn't reach their ends.
Inputs may be any that keep to these rules, and one draw needn't show every extreme that they name: `stretch_owner`: every entry is a multiple of 16; the passage's tile t lies on owner stretch_owner + t, counting owners seq-major over seq and req. `recomp`: the entries of one passage's list that are not -1 differ from each other.
All inputs are finite; a program needn't handle non-finite values.
Results may differ from the reference program's by a relative error of at most 0.0049.
Values may be sent and summed in bfloat16 or wider, within the bound.
A program may use at most 64 MiB of HBM per device.

```python
import jax
import jax.numpy as jnp
from jax import lax

QH = 96
KVH = 8
HD = 128
TILE = 128
STRETCH = 2048
RPC = 1
PS = 16
REQS = 32
NOWN = 64
TPC = 16
OWN_BLK = 16
ROWS = 256
CTX = 4096
N_SEQ = 2
N_REQ = 32


def shared_fresh(key):
    normals = jax.random.normal(jax.random.fold_in(key, 11), (REQS, KVH, ROWS, 2 * HD), jnp.float32)
    normals = jnp.clip(normals, -6.0, 6.0)
    return normals


def draw_fresh_kv(key, part):
    fresh = shared_fresh(key)
    return fresh.astype(jnp.bfloat16)


def draw_queries(key, part):
    key = jax.random.fold_in(key, 22)
    drawn = jnp.clip(jax.random.normal(key, (REQS, ROWS, QH * HD), jnp.float32), -6.0, 6.0)
    return drawn.astype(jnp.bfloat16)


def draw_stretch_owner(key, part):
    key = jax.random.fold_in(key, 3)
    blocks = NOWN // OWN_BLK
    chosen = jax.random.randint(key, (REQS, N_SEQ), 0, blocks, jnp.int32)
    chosen = chosen.at[REQS - 1, N_SEQ - 1].set(blocks - 1)
    chosen = chosen.at[REQS - 1, 0].set(0)
    chosen = chosen.at[0, 0].set(NOWN // 2 // OWN_BLK)
    return (chosen * OWN_BLK).astype(jnp.int32)


def draw_recomp(key, part):
    key = jax.random.fold_in(key, 5)
    first_tile = jax.random.randint(jax.random.fold_in(key, 1), (REQS, N_SEQ, 1), 0, TPC, jnp.int32)
    tiles = (first_tile + jnp.arange(RPC, dtype=jnp.int32)[None, None, :]) % TPC
    kept = jax.random.randint(jax.random.fold_in(key, 2), (REQS, N_SEQ, RPC), 0, 3, jnp.int32) > 0
    entries = jnp.where(kept, tiles, -1)
    last_tiles = (TPC - 1 + jnp.arange(RPC, dtype=jnp.int32)) % TPC
    entries = entries.at[0, 0, :].set(last_tiles)
    entries = entries.at[0, N_SEQ - 1, :].set(last_tiles)
    entries = entries.at[REQS - 1, 0, :].set(-1)
    return entries.astype(jnp.int32)


def plant(array, rng, least, largest):
    shape = array.shape
    place = [jax.random.randint(jax.random.fold_in(rng, axis), (), 0, shape[axis]) for axis in range(len(shape))]
    array = array.at[tuple(place)].set(least)
    longest = shape.index(max(shape))
    place[longest] = (place[longest] + 1) % shape[longest]
    return array.at[tuple(place)].set(largest)


def block_scale(rng, shape, shards, smallest, top_value):
    gain, own = 1.0, jax.random.fold_in(rng, 6)
    for dim, parts in shards:
        steps = jnp.exp(jax.random.uniform(jax.random.fold_in(own, dim), (parts,), jnp.float32, smallest / len(shards), top_value / len(shards)))
        gain = gain * jnp.repeat(steps, shape[dim] // parts).reshape([-1 if axis == dim else 1 for axis in range(len(shape))])
    return gain


def gaussian(key, extent, scale, bound, cuts=(), kind=jnp.bfloat16):
    values = scale * jax.random.normal(key, extent, jnp.float32)
    if cuts:
        values = values * block_scale(key, extent, cuts, -0.22, 0.18)
    return jnp.clip(values, -bound, bound).astype(kind)


def setup_inputs(seed: int = 0) -> dict:
    seeds = jax.random.split(jax.random.key(seed), 7)
    cache_pool = gaussian(seeds[0], (N_SEQ, N_REQ, KVH, PS, TILE, 2 * HD), 1.0, 6.0, ((0, 2), (1, 32), (2, 4)))
    fresh_kv = draw_fresh_kv(jax.random.fold_in(seeds[6], 71), 0)
    queries = draw_queries(jax.random.fold_in(seeds[6], 71), 0)
    stretch_owner = draw_stretch_owner(jax.random.fold_in(seeds[6], 71), 0)
    stretch_slot = plant(jax.random.randint(seeds[4], (REQS, N_SEQ), 0, PS), jax.random.fold_in(seeds[4], 1), 0, PS - 1).astype(jnp.int32)
    recomp = draw_recomp(jax.random.fold_in(seeds[6], 71), 0)
    return dict(cache_pool=cache_pool, fresh_kv=fresh_kv, queries=queries, stretch_owner=stretch_owner, stretch_slot=stretch_slot, recomp=recomp)


def reference(cache_pool, fresh_kv, queries, stretch_owner, stretch_slot, recomp):
    tiles_span = STRETCH // TILE
    owner_span = tiles_span
    pool_flat = cache_pool.reshape(N_SEQ * N_REQ, KVH, PS, TILE, 2 * HD)
    owners = stretch_owner[:, :, None] + jnp.arange(owner_span, dtype=jnp.int32)[None, None, :]
    slot_ids = jnp.broadcast_to(stretch_slot[:, :, None], owners.shape)
    cached = pool_flat[owners, :, slot_ids]
    cached = jnp.transpose(cached, (0, 3, 1, 2, 4, 5))
    cached = cached.reshape(REQS, KVH, N_SEQ, tiles_span, TILE, 2 * HD)
    matches = recomp[:, :, :, None] == jnp.arange(tiles_span, dtype=jnp.int32)[None, None, None, :]
    present = jnp.any(matches, axis=2)
    slot_of = jnp.sum(matches.astype(jnp.int32) * jnp.arange(RPC, dtype=jnp.int32)[None, None, :, None], axis=2)
    fresh = fresh_kv.reshape(REQS, KVH, N_SEQ, RPC, TILE, 2 * HD)
    replaced = jnp.take_along_axis(fresh, slot_of[:, None, :, :, None, None], axis=3)
    blended = jnp.where(present[:, None, :, :, None, None], replaced, cached)
    is_live = recomp >= 0
    tile_pick = jnp.maximum(recomp, 0).astype(jnp.int32)
    chosen = jnp.take_along_axis(cached, tile_pick[:, None, :, :, None, None], axis=3)
    difference = fresh.astype(jnp.float32) - chosen.astype(jnp.float32)
    squared = jnp.sum(difference * difference, axis=(1, 5)) / (2 * KVH * HD)
    deviation = (squared * is_live[:, :, :, None].astype(jnp.float32)).reshape(REQS, ROWS)

    keys_all = blended.reshape(REQS, KVH, CTX, 2 * HD)
    q_all = queries.reshape(REQS, N_SEQ * RPC, TILE, KVH, QH // KVH, HD)
    q_start = (jnp.arange(N_SEQ, dtype=jnp.int32)[None, :, None] * STRETCH + tile_pick * TILE).reshape(REQS, N_SEQ * RPC)
    key_pos = jnp.arange(CTX, dtype=jnp.int32)
    row_pos = jnp.arange(TILE, dtype=jnp.int32)

    def one_tile(flat_index):
        request = flat_index // (N_SEQ * RPC)
        slot_no = flat_index % (N_SEQ * RPC)
        q_tile = q_all[request, slot_no]
        first_pos = q_start[request, slot_no]
        visible = key_pos[None, :] <= first_pos + row_pos[:, None]
        context = keys_all[request]

        def one_head(kv_head):
            q_head = q_tile[:, kv_head].astype(jnp.float32)
            key_rows = context[kv_head, :, :HD].astype(jnp.float32)
            value_rows = context[kv_head, :, HD:].astype(jnp.float32)
            scores = jnp.einsum('tgd,kd->gtk', q_head, key_rows) * (HD ** -0.5)
            scores = jnp.where(visible[None], scores, -jnp.inf)
            row_max = jnp.max(scores, axis=-1, keepdims=True)
            expo = jnp.exp(scores - row_max)
            weights = lax.optimization_barrier(expo.astype(jnp.bfloat16)).astype(jnp.float32)
            result = jnp.einsum('gtk,kd->gtd', weights, value_rows) / jnp.sum(expo, axis=-1)[:, :, None]
            return jnp.transpose(result, (1, 0, 2))

        heads = lax.map(one_head, jnp.arange(KVH, dtype=jnp.int32))
        return jnp.transpose(heads, (1, 0, 2, 3)).reshape(TILE, QH * HD)

    tiles_out = lax.map(one_tile, jnp.arange(REQS * N_SEQ * RPC, dtype=jnp.int32))
    tiles_out = tiles_out * is_live.reshape(REQS * N_SEQ * RPC)[:, None, None].astype(tiles_out.dtype)
    attended = tiles_out.reshape(REQS, ROWS, QH * HD).astype(jnp.bfloat16)
    return attended, deviation
```

```python
import functools

import jax
import jax.numpy as jnp
import numpy as np
from jax import lax
from jax.experimental import pallas as pl
from jax.experimental.pallas import tpu as pltpu
from jax.sharding import PartitionSpec as P

KVH = 8
HD = 128
TILE = 128
NT = 16
PER_KV = 12
HCOLS = PER_KV * HD
NZ = 8
NY = 4
MESH = pl.DeviceIdType.MESH
LOG2E = 1.4426950408889634
LEVELS = ((14, 10, 7, 3), (17, 13, 8, 4), (20, 15, 10, 4), (28, 20, 12, 4))


def need_weights():
    weights = np.zeros((4, 2, NZ, NZ, NY, 2), np.int32)
    for hop in range(1, 5):
        for way, sign in ((0, 1), (1, -1)):
            for k in range(NZ):
                for d in range(hop, 5):
                    for y in range(NY):
                        if d < 4 or y % 2 == way:
                            weights[hop - 1, way, k, (k + sign * d) % NZ, y] = 1
    return weights.reshape(4, 2, NZ, NZ * NY * 2)


def tables_kernel(tiles, half, entry, tab):
    me = lax.axis_index("req")
    z, y = me // NY, lax.rem(me, NY)

    def wanted(place, k):
        tile = NY * lax.rem(k, 4) + y
        return jnp.where((half[place] == k // 4) & (tiles[place] > tile), 1, 0)

    def columns(d, way):
        return [q for q in range(2 * NY) if d < 4 or (q // 2) % 2 == way]

    for way, sign in ((0, 1), (1, -1)):
        place = jnp.int32(0)
        for slot in range(32):
            tab[way * 32 + slot] = 0
        for d in (4, 3, 2, 1):
            row = lax.rem(z + sign * d + NZ, NZ)
            for q in columns(d, way):
                tab[way * 32 + place] = entry[row * 8 + q]
                place = place + wanted(row * 8 + q, z)
    for j in range(4):
        counts = []
        for way, sign in ((0, 1), (1, -1)):
            far = (j if way == 0 else 4 - j) if j else 4
            k = lax.rem(z - sign * far + NZ, NZ)
            count = jnp.int32(0)
            for d in range(4, far, -1):
                row = lax.rem(k + sign * d + NZ, NZ)
                for q in columns(d, way):
                    count = count + wanted(row * 8 + q, k)
            counts.append((k, count))
        for q in range(2 * NY):
            here = z * 8 + q
            if j:
                (kf, cf), (kb, cb) = counts
                wf, wb = wanted(here, kf), wanted(here, kb)
                tab[64 + j * 8 + q] = cf * wf + cb * wb
                tab[96 + j * 8 + q] = wb
                counts = [(kf, cf + wf), (kb, cb + wb)]
            else:
                way = (q // 2) % 2
                k, count = counts[way]
                w = wanted(here, k)
                tab[64 + q] = jnp.where(w > 0, count, entry[here])
                tab[96 + q] = w
                counts[way] = (k, count + w)


def comm_kernel(
    caps, chunk, tab, pool, fresh, q, ctx, qx, fx,
    poolbuf, stage, r1, r2, r3, r4, yst,
    zsend, zrecv, ysend, yrecv, xsend, xrecv, lsem,
):
    s = lax.axis_index("seq")
    x = lax.axis_index("tp")
    me = lax.axis_index("req")
    z, y = me // NY, lax.rem(me, NY)
    p1, p2, p3, p4 = caps
    core = (1 - s, x, me)
    zdev = [(s, x, lax.rem(z + 1, NZ) * NY + y), (s, x, lax.rem(z + NZ - 1, NZ) * NY + y)]
    ydev = [(s, x, z * NY + lax.rem(y + dy, NY)) for dy in (1, 2, 3)]

    barrier = pltpu.get_barrier_semaphore()
    for device in [core] + zdev + ydev:
        pl.semaphore_signal(barrier, inc=1, device_id=device, device_id_type=MESH)
    pl.semaphore_wait(barrier, 6)

    other = pl.ds(pl.multiple_of((1 - s) * HCOLS, HCOLS), HCOLS)
    mine = pl.ds(pl.multiple_of(s * HCOLS, HCOLS), HCOLS)
    swaps = [(pool.at[1 - s], poolbuf.at[s]), (q.at[:, other], qx.at[s]), (fresh.at[1 - s], fx.at[s])]
    keeps = [(pool.at[s], poolbuf.at[s]), (q.at[:, mine], qx.at[s]), (fresh.at[s], fx.at[s])]
    swaps = [
        pltpu.make_async_remote_copy(
            src_ref=src, dst_ref=dst, send_sem=xsend.at[i], recv_sem=xrecv.at[i],
            device_id=core, device_id_type=MESH,
        )
        for i, (src, dst) in enumerate(swaps)
    ]
    keeps = [pltpu.make_async_copy(src, dst, lsem.at[i]) for i, (src, dst) in enumerate(keeps)]
    for i in range(3):
        swaps[i].start()
        keeps[i].start()
    keeps[0].wait()
    swaps[0].wait()

    buffers = [
        [(stage.at[0], 0), (r1, 0), (r2, 0), (r3, 0), (r4, 0)],
        [(stage.at[1], 0), (r3, p3), (r2, p2), (r1, p1), (r4, p4)],
    ]

    def zcopy(hop, way, i):
        low = i * chunk
        size = min(chunk, caps[hop - 1] - low)
        src, src_at = buffers[way][hop - 1]
        dst, dst_at = buffers[way][hop]
        return pltpu.make_async_remote_copy(
            src_ref=src.at[pl.ds(src_at + low, size)],
            dst_ref=dst.at[pl.ds(dst_at + low, size)],
            send_sem=zsend.at[hop - 1, way, i],
            recv_sem=zrecv.at[hop - 1, way, i],
            device_id=zdev[way],
            device_id_type=MESH,
        )

    def chunks(hop):
        return -(-caps[hop - 1] // chunk)

    for i in range(chunks(1)):
        for way in range(2):
            for place in range(i * chunk, min((i + 1) * chunk, p1)):
                row = tab[way * 32 + place]
                stage[way, place] = poolbuf[row // NT, lax.rem(row, NT)]
            zcopy(1, way, i).start()

    def ycopy(j, dy):
        tile = NY * lax.rem(z - j + NZ, 4) + y
        return pltpu.make_async_remote_copy(
            src_ref=yst.at[j, dy - 1],
            dst_ref=ctx.at[tile],
            send_sem=ysend.at[j, dy - 1],
            recv_sem=yrecv.at[j, dy - 1],
            device_id=ydev[dy - 1],
            device_id_type=MESH,
        )

    def hand_out(j):
        def picked(column, c):
            at = j * 8 + column * 2 + c
            place, side = tab[64 + at], tab[96 + at]
            if j:
                return (r1, r2, r3)[j - 1][place + side * caps[j - 1]]
            near = jnp.where(side > 0, 0, place)
            far = jnp.where(side > 0, place, 0)
            far = far + lax.rem(column, 2) * p4
            local = poolbuf[near // NT, lax.rem(near, NT)]
            return jnp.where(side > 0, r4[far], local)

        for dy in (2, 1, 3):
            column = lax.rem(y + dy, NY)
            for c in range(2):
                yst[j, dy - 1, c] = picked(column, c)
            ycopy(j, dy).start()
        tile = NY * lax.rem(z - j + NZ, 4) + y
        for c in range(2):
            ctx[tile, c] = picked(y, c)

    for hop in (2, 3, 4):
        for i in range(chunks(hop - 1)):
            for way in range(2):
                zcopy(hop - 1, way, i).wait_recv()
                if i < chunks(hop):
                    zcopy(hop, way, i).start()
        if hop == 3:
            hand_out(2)
        if hop == 4:
            hand_out(1)
            hand_out(3)
    for i in range(chunks(4)):
        for way in range(2):
            zcopy(4, way, i).wait_recv()
    hand_out(0)

    for j in range(4):
        for dy in (1, 2, 3):
            ycopy(j, dy).wait()
    for hop in (1, 2, 3, 4):
        for i in range(chunks(hop)):
            for way in range(2):
                zcopy(hop, way, i).wait_send()
    for i in (1, 2):
        keeps[i].wait()
        swaps[i].wait()


def comm_call(level, tab, pool, fresh, q):
    caps = LEVELS[level]
    chunk = 2 if level < len(LEVELS) - 1 else 4
    p1, p2, p3, p4 = caps
    most = -(-p1 // chunk)
    tile = (TILE, 2 * HD)
    bf = jnp.bfloat16
    anyspace = pl.BlockSpec(memory_space=pl.ANY)
    return pl.pallas_call(
        functools.partial(comm_kernel, caps, chunk),
        out_shape=(
            jax.ShapeDtypeStruct((NT, 2) + tile, bf),
            jax.ShapeDtypeStruct((2, TILE, HCOLS), bf),
            jax.ShapeDtypeStruct((2,) + tile, bf),
        ),
        in_specs=[pl.BlockSpec(memory_space=pltpu.SMEM), anyspace, anyspace, anyspace],
        out_specs=(pl.BlockSpec(memory_space=pltpu.VMEM), anyspace, anyspace),
        scratch_shapes=[
            pltpu.VMEM((2, NT) + tile, bf),
            pltpu.VMEM((2, p1) + tile, bf),
            pltpu.VMEM((p1 + p3,) + tile, bf),
            pltpu.VMEM((2 * p2,) + tile, bf),
            pltpu.VMEM((p3 + p1,) + tile, bf),
            pltpu.VMEM((2 * p4,) + tile, bf),
            pltpu.VMEM((4, 3, 2) + tile, bf),
            pltpu.SemaphoreType.DMA((4, 2, most)),
            pltpu.SemaphoreType.DMA((4, 2, most)),
            pltpu.SemaphoreType.DMA((4, 3)),
            pltpu.SemaphoreType.DMA((4, 3)),
            pltpu.SemaphoreType.DMA((3,)),
            pltpu.SemaphoreType.DMA((3,)),
            pltpu.SemaphoreType.DMA((3,)),
        ],
        compiler_params=pltpu.CompilerParams(
            collective_id=1 + level, has_side_effects=True, vmem_limit_bytes=40 * 2**20
        ),
    )(tab, pool, fresh, q)


def attend_kernel(rec, ctx, qx, fx, out, dev, keys, values):
    scale = HD**-0.5 * LOG2E
    for c in range(2):
        entry = rec[c]
        own = fx[c]

        def blend(t, carry):
            tile = jnp.where(t == entry, own, ctx[t, c])
            rows = pl.ds(pl.multiple_of(t * TILE, TILE), TILE)
            keys[c, rows] = tile[:, :HD]
            values[c, rows, :HD] = jnp.ones((TILE, HD), jnp.bfloat16)
            values[c, rows, HD:] = tile[:, HD:]
            return carry

        lax.fori_loop(0, NT, blend, 0)
        cached = ctx[jnp.maximum(entry, 0), c].astype(jnp.float32)
        gap = own.astype(jnp.float32) - cached
        gap = gap * gap
        gap = jnp.transpose(gap[:, :HD] + gap[:, HD:])
        total = jnp.sum(gap, axis=0, keepdims=True) / (2 * KVH * HD)
        dev[c : c + 1] = jnp.where(entry >= 0, total, 0.0)
    dev[2:8] = jnp.zeros((6, TILE), jnp.float32)

    width = 2 * HD

    def scores(slot, c, block):
        raw = lax.dot_general(
            block, keys[c], (((1,), (1,)), ((), ())), preferred_element_type=jnp.float32
        )
        if slot != c:
            return raw
        last = jnp.maximum(rec[c], 0) * TILE + lax.rem(lax.broadcasted_iota(jnp.int32, raw.shape, 0), TILE)
        at = lax.broadcasted_iota(jnp.int32, raw.shape, 1)
        return jnp.where(at <= last, raw, -1e30)

    for slot in range(2):

        def group(i, carry):
            cols = pl.ds(pl.multiple_of(i * width, width), width)
            pair = qx[slot, :, cols]
            block = jnp.concatenate([pair[:, :HD], pair[:, HD:]], axis=0)
            parts = [scores(slot, c, block) for c in range(slot + 1)]
            top = functools.reduce(jnp.maximum, [jnp.max(p, axis=1, keepdims=True) for p in parts])
            total = jnp.zeros((2 * TILE, 2 * HD), jnp.float32)
            for c in range(slot + 1):
                weights = jnp.exp2((parts[c] - top) * scale).astype(jnp.bfloat16)
                total += jnp.dot(weights, values[c], preferred_element_type=jnp.float32)
            result = total[:, HD:] / total[:, :HD]
            result = jnp.where(rec[slot] >= 0, result, 0.0).astype(jnp.bfloat16)
            out[slot, :, cols] = jnp.concatenate([result[:TILE], result[TILE:]], axis=1)
            return carry

        lax.fori_loop(0, PER_KV // 2, group, 0)


def attend_call(rec, ctx, qx, fx):
    vmem = pl.BlockSpec(memory_space=pltpu.VMEM)
    return pl.pallas_call(
        attend_kernel,
        out_shape=(
            jax.ShapeDtypeStruct((2, TILE, HCOLS), jnp.bfloat16),
            jax.ShapeDtypeStruct((8, TILE), jnp.float32),
        ),
        in_specs=[pl.BlockSpec(memory_space=pltpu.SMEM), vmem, vmem, vmem],
        out_specs=(vmem, vmem),
        scratch_shapes=[
            pltpu.VMEM((2, NT * TILE, HD), jnp.bfloat16),
            pltpu.VMEM((2, NT * TILE, 2 * HD), jnp.bfloat16),
        ],
        compiler_params=pltpu.CompilerParams(vmem_limit_bytes=48 * 2**20),
    )(rec, ctx, qx, fx)


def return_kernel(o, devp, out, dev, gathered, osend, orecv, dsend, drecv, lsem):
    s = lax.axis_index("seq")
    x = lax.axis_index("tp")
    me = lax.axis_index("req")
    peers = [(lax.rem(s + ds, 2), lax.rem(x + dx, 4), me) for ds in range(2) for dx in range(4)][1:]
    barrier = pltpu.get_barrier_semaphore()
    for device in peers:
        pl.semaphore_signal(barrier, inc=1, device_id=device, device_id_type=MESH)
    pl.semaphore_wait(barrier, 7)
    mine = pl.ds(pl.multiple_of(s * HCOLS, HCOLS), HCOLS)
    swap = pltpu.make_async_remote_copy(
        src_ref=o.at[1 - s], dst_ref=out.at[:, mine], send_sem=osend, recv_sem=orecv,
        device_id=(1 - s, x, me), device_id_type=MESH,
    )
    swap.start()
    sends = []
    for i, device in enumerate(peers):
        sends.append(
            pltpu.make_async_remote_copy(
                src_ref=devp, dst_ref=gathered.at[i], send_sem=dsend.at[i], recv_sem=drecv.at[i],
                device_id=device, device_id_type=MESH,
            )
        )
        sends[-1].start()
    keep = pltpu.make_async_copy(o.at[s], out.at[:, mine], lsem)
    keep.start()
    total = devp[...]
    for i in range(7):
        sends[i].wait()
        total = total + gathered[i]
    dev[...] = jnp.where(s == 0, total[0:1], total[1:2])
    keep.wait()
    swap.wait()


def return_call(o, devp):
    vmem = pl.BlockSpec(memory_space=pltpu.VMEM)
    return pl.pallas_call(
        return_kernel,
        out_shape=(
            jax.ShapeDtypeStruct((TILE, 2 * HCOLS), jnp.bfloat16),
            jax.ShapeDtypeStruct((1, TILE), jnp.float32),
        ),
        in_specs=[vmem, vmem],
        out_specs=(vmem, vmem),
        scratch_shapes=[
            pltpu.VMEM((7, 8, TILE), jnp.float32),
            pltpu.SemaphoreType.DMA,
            pltpu.SemaphoreType.DMA,
            pltpu.SemaphoreType.DMA((7,)),
            pltpu.SemaphoreType.DMA((7,)),
            pltpu.SemaphoreType.DMA,
        ],
        compiler_params=pltpu.CompilerParams(
            collective_id=0, has_side_effects=True, vmem_limit_bytes=16 * 2**20
        ),
    )(o, devp)


def on_device(cache_pool, fresh_kv, queries, stretch_owner, stretch_slot, recomp):
    entries = recomp[:, :, 0]
    live = entries >= 0
    reach = jnp.where(live, entries + 1, 0)
    tiles = jnp.stack([jnp.where(live[:, 1], NT, reach[:, 0]), reach[:, 1]], axis=1).reshape(-1)
    half = lax.rem(stretch_owner // NT, 2).reshape(-1)
    entry = ((stretch_owner // (2 * NT)) * NT + stretch_slot).reshape(-1)

    rows = jnp.arange(NZ, dtype=jnp.int32)[:, None]
    wanted = ((half[None] == rows // 4) & (tiles[None] > NY * (rows % 4))).astype(jnp.int32)
    need = jnp.max(jnp.sum(wanted[None, None] * need_weights(), axis=-1), axis=(1, 2))
    level = jnp.int32(0)
    for caps in LEVELS[:-1]:
        level = level + jnp.any(need > np.array(caps, np.int32)).astype(jnp.int32)

    smem = pl.BlockSpec(memory_space=pltpu.SMEM)
    tab = pl.pallas_call(
        tables_kernel,
        out_shape=jax.ShapeDtypeStruct((128,), jnp.int32),
        in_specs=[smem] * 3,
        out_specs=smem,
    )(tiles, half, entry)
    ctx, qx, fx = lax.switch(
        level,
        [functools.partial(comm_call, i) for i in range(len(LEVELS))],
        tab, cache_pool[0, 0], fresh_kv[0], queries[0],
    )
    rec = lax.dynamic_index_in_dim(entries, lax.axis_index("req"), 0, keepdims=False)
    o, devp = attend_call(rec, ctx, qx, fx)
    out, dev = return_call(o, devp)
    return out[None], dev


def solution(mesh):
    placed = (
        P("seq", "req", "tp", None, None, None),
        P("req", "tp", "seq", None),
        P("req", "seq", "tp"),
        P(),
        P(),
        P(),
    )
    return jax.shard_map(
        on_device,
        mesh=mesh,
        in_specs=placed,
        out_specs=(P("req", "seq", "tp"), P("req", "seq")),
        check_vma=False,
    )
```

```python
import functools

import jax
import jax.numpy as jnp
import numpy as np
from jax import lax
from jax.experimental import pallas as pl
from jax.experimental.pallas import tpu as pltpu
from jax.sharding import PartitionSpec as P

KVH = 8
HD = 128
TILE = 128
NT = 16
PER_KV = 12
HCOLS = PER_KV * HD
NZ = 8
NY = 4
MESH = pl.DeviceIdType.MESH
SCALE = HD**-0.5 * 1.4426950408889634
LOW = -1e30
LEVELS = ((14, 10, 7, 3), (17, 13, 8, 4), (20, 15, 10, 4), (28, 20, 12, 4))


def need_weights():
    weights = np.zeros((4, 2, NZ, NZ, NY, 2), np.int32)
    for hop in range(1, 5):
        for way, sign in ((0, 1), (1, -1)):
            for k in range(NZ):
                for d in range(hop, 5):
                    for y in range(NY):
                        if d < 4 or y % 2 == way:
                            weights[hop - 1, way, k, (k + sign * d) % NZ, y] = 1
    return weights.reshape(4, 2, NZ, NZ * NY * 2)


def tables_kernel(tiles, half, entry, tab):
    me = lax.axis_index("req")
    z, y = me // NY, lax.rem(me, NY)

    def wanted(place, k):
        tile = NY * lax.rem(k, 4) + y
        return jnp.where((half[place] == k // 4) & (tiles[place] > tile), 1, 0)

    def columns(d, way):
        return [q for q in range(2 * NY) if d < 4 or (q // 2) % 2 == way]

    for way, sign in ((0, 1), (1, -1)):
        place = jnp.int32(0)
        for slot in range(32):
            tab[way * 32 + slot] = 0
        for d in (4, 3, 2, 1):
            row = lax.rem(z + sign * d + NZ, NZ)
            for q in columns(d, way):
                tab[way * 32 + place] = entry[row * 8 + q]
                place = place + wanted(row * 8 + q, z)
    for j in range(4):
        counts = []
        for way, sign in ((0, 1), (1, -1)):
            far = (j if way == 0 else 4 - j) if j else 4
            k = lax.rem(z - sign * far + NZ, NZ)
            count = jnp.int32(0)
            for d in range(4, far, -1):
                row = lax.rem(k + sign * d + NZ, NZ)
                for q in columns(d, way):
                    count = count + wanted(row * 8 + q, k)
            counts.append((k, count))
        for q in range(2 * NY):
            here = z * 8 + q
            if j:
                (kf, cf), (kb, cb) = counts
                wf, wb = wanted(here, kf), wanted(here, kb)
                tab[64 + j * 8 + q] = cf * wf + cb * wb
                tab[96 + j * 8 + q] = wb
                counts = [(kf, cf + wf), (kb, cb + wb)]
            else:
                way = (q // 2) % 2
                k, count = counts[way]
                w = wanted(here, k)
                tab[64 + q] = jnp.where(w > 0, count, entry[here])
                tab[96 + q] = w
                counts[way] = (k, count + w)


def segments(caps):
    p1, p2, p3, p4 = caps
    head = [
        (1, 0, p4), (1, p4, p3), (2, 0, p4), (1, p3, p2), (3, 0, p4),
        (2, p4, p3), (4, 0, p4), (2, p3, p2),
    ]
    near, far = (1, p2, p1), (3, p4, p3)
    return [[piece for piece in order if piece[1] < piece[2]] for order in (head + [near, far], head + [far, near])]


def whole_kernel(
    caps, tab, rec, pool, fresh, q, out, dev,
    qx, fx, poolbuf, stage, r1, r2, r3, r4, yst, ctx,
    qs, kt, vs, top, acc, ost, devp, gathered,
    zsend, zrecv, ysend, yrecv, xsend, xrecv, lsem, dsend, drecv, osend, orecv, osem,
):
    s = lax.axis_index("seq")
    x = lax.axis_index("tp")
    me = lax.axis_index("req")
    z, y = me // NY, lax.rem(me, NY)
    p1, p2, p3, p4 = caps
    zdev = [(s, x, lax.rem(z + 1, NZ) * NY + y), (s, x, lax.rem(z + NZ - 1, NZ) * NY + y)]
    ydev = [(s, x, z * NY + lax.rem(y + dy, NY)) for dy in (1, 2, 3)]
    peers = [(lax.rem(s + ds, 2), lax.rem(x + dx, 4), me) for ds in range(2) for dx in range(4)][1:]
    core = peers[3]

    barrier = pltpu.get_barrier_semaphore()
    for device in peers + zdev + ydev:
        pl.semaphore_signal(barrier, inc=1, device_id=device, device_id_type=MESH)
    pl.semaphore_wait(barrier, len(peers + zdev + ydev))

    other = pl.ds(pl.multiple_of((1 - s) * HCOLS, HCOLS), HCOLS)
    mine = pl.ds(pl.multiple_of(s * HCOLS, HCOLS), HCOLS)
    swaps = [(pool.at[1 - s], poolbuf.at[s]), (q.at[:, other], qx.at[s]), (fresh.at[1 - s], fx.at[s])]
    keeps = [(pool.at[s], poolbuf.at[s]), (q.at[:, mine], qx.at[s]), (fresh.at[s], fx.at[s])]
    swaps = [
        pltpu.make_async_remote_copy(
            src_ref=src, dst_ref=dst, send_sem=xsend.at[i], recv_sem=xrecv.at[i],
            device_id=core, device_id_type=MESH,
        )
        for i, (src, dst) in enumerate(swaps)
    ]
    keeps = [pltpu.make_async_copy(src, dst, lsem.at[i]) for i, (src, dst) in enumerate(keeps)]
    for i in range(3):
        swaps[i].start()
        keeps[i].start()
    keeps[0].wait()
    swaps[0].wait()

    buffers = [
        [(stage.at[0], 0), (r1, 0), (r2, 0), (r3, 0), (r4, 0)],
        [(stage.at[1], 0), (r3, p3), (r2, p2), (r1, p1), (r4, p4)],
    ]
    orders = segments(caps)
    index = [{piece: i for i, piece in enumerate(order)} for order in orders]

    def zcopy(way, piece):
        hop, low, high = piece
        src, src_at = buffers[way][hop - 1]
        dst, dst_at = buffers[way][hop]
        i = index[way][piece]
        return pltpu.make_async_remote_copy(
            src_ref=src.at[pl.ds(src_at + low, high - low)],
            dst_ref=dst.at[pl.ds(dst_at + low, high - low)],
            send_sem=zsend.at[way, i],
            recv_sem=zrecv.at[way, i],
            device_id=zdev[way],
            device_id_type=MESH,
        )

    for step in range(len(orders[0])):
        for way in range(2):
            hop, low, high = piece = orders[way][step]
            if hop == 1:

                def fetch(place, carry):
                    row = tab[way * 32 + place]
                    stage[way, place] = poolbuf[row // NT, lax.rem(row, NT)]
                    return carry

                lax.fori_loop(low, high, fetch, 0)
            else:
                zcopy(way, (hop - 1, low, high)).wait_recv()
            zcopy(way, piece).start()
        if step == 2:
            for i in (1, 2):
                keeps[i].wait()
                swaps[i].wait()
            eye = jnp.where(
                lax.broadcasted_iota(jnp.int32, (TILE, TILE), 0)
                == lax.broadcasted_iota(jnp.int32, (TILE, TILE), 1),
                1.0,
                0.0,
            ).astype(jnp.bfloat16)
            for slot in range(2):
                for g in range(PER_KV):
                    qs[slot, g * TILE : (g + 1) * TILE, :HD] = qx[slot, :, g * HD : (g + 1) * HD]
                    qs[slot, g * TILE : (g + 1) * TILE, HD:] = eye
            vs[...] = jnp.ones(vs.shape, vs.dtype)
            top[...] = jnp.full(top.shape, LOW, top.dtype)
            acc[...] = jnp.zeros(acc.shape, acc.dtype)

    def group(j):
        return lax.rem(z - j + NZ, 4)

    def ycopy(j, dy):
        return pltpu.make_async_remote_copy(
            src_ref=yst.at[j, dy - 1],
            dst_ref=ctx.at[NY * group(j) + y],
            send_sem=ysend.at[j, dy - 1],
            recv_sem=yrecv.at[j, dy - 1],
            device_id=ydev[dy - 1],
            device_id_type=MESH,
        )

    def hand_out(j):
        for way in range(2):
            last = [(4, 0, p4), (1, p2, p1), (2, p3, p2), (3, p4, p3)]
            piece = last[j if way == 0 else (4 - j) % 4]
            if piece in index[way]:
                zcopy(way, piece).wait_recv()

        def picked(column, c):
            at = j * 8 + column * 2 + c
            place, side = tab[64 + at], tab[96 + at]
            if j:
                return (r1, r2, r3)[j - 1][place + side * caps[j - 1]]
            near = jnp.where(side > 0, 0, place)
            far = jnp.where(side > 0, place, 0)
            far = far + lax.rem(column, 2) * p4
            local = poolbuf[near // NT, lax.rem(near, NT)]
            return jnp.where(side > 0, r4[far], local)

        for dy in (2, 1, 3):
            column = lax.rem(y + dy, NY)
            for c in range(2):
                yst[j, dy - 1, c] = picked(column, c)
            ycopy(j, dy).start()
        for c in range(2):
            ctx[NY * group(j) + y, c] = picked(y, c)

    def arrived(j):
        for dy in (1, 2, 3):
            ycopy(j, dy).wait_recv()

    def attend(j):
        for c in range(2):
            entry = rec[c]
            last = jnp.maximum(entry, 0) * TILE + lax.broadcasted_iota(jnp.int32, (TILE, TILE), 0)
            for i in range(NY):
                t = NY * group(j) + i
                tile = jnp.where(t == entry, fx[c], ctx[t, c])
                cols = slice(i * TILE, (i + 1) * TILE)
                kt[c, :HD, cols] = jnp.transpose(tile[:, :HD])
                vs[c, cols, HD:] = tile[:, HD:]
                at = t * TILE + lax.broadcasted_iota(jnp.int32, (TILE, TILE), 1)
                kt[c, HD:, cols] = jnp.where(at <= last, 0.0, LOW).astype(jnp.bfloat16)
        for slot in range(2):

            def block(i, carry):
                rows = pl.ds(pl.multiple_of(i * 2 * TILE, 2 * TILE), 2 * TILE)
                qq = qs[slot, rows]
                parts = [jnp.dot(qq, kt[slot], preferred_element_type=jnp.float32)]
                if slot:
                    parts.append(jnp.dot(qq[:, :HD], kt[0, :HD], preferred_element_type=jnp.float32))
                peak = functools.reduce(
                    jnp.maximum, [part[:, i * HD : (i + 1) * HD] for part in parts for i in range(NY)]
                )
                old = top[slot, rows]
                new = jnp.maximum(old, jnp.max(peak, axis=1, keepdims=True))
                top[slot, rows] = new
                wide = jnp.concatenate([new] * NY, axis=1)
                factor = jnp.exp2((old - new) * SCALE)
                total = acc[slot, rows] * jnp.concatenate([factor, factor], axis=1)
                for part, c in zip(parts, (slot, 0)):
                    weights = jnp.exp2((part - wide) * SCALE).astype(jnp.bfloat16)
                    total = total + jnp.dot(weights, vs[c], preferred_element_type=jnp.float32)
                acc[slot, rows] = total
                return carry

            lax.fori_loop(0, PER_KV // 2, block, 0, unroll=PER_KV // 2)

    hand_out(0)
    hand_out(2)
    hand_out(1)
    arrived(0)
    attend(0)
    hand_out(3)
    arrived(2)
    attend(2)
    arrived(1)
    attend(1)
    arrived(3)

    devp[...] = jnp.zeros(devp.shape, devp.dtype)
    for c in range(2):
        entry = rec[c]
        gap = fx[c].astype(jnp.float32) - ctx[jnp.maximum(entry, 0), c].astype(jnp.float32)
        gap = gap * gap
        gap = jnp.transpose(gap[:, :HD] + gap[:, HD:])
        total = jnp.sum(gap, axis=0, keepdims=True) / (2 * KVH * HD)
        devp[c : c + 1] = jnp.where(entry >= 0, total, 0.0)
    sends = []
    for i, device in enumerate(peers):
        sends.append(
            pltpu.make_async_remote_copy(
                src_ref=devp, dst_ref=gathered.at[i], send_sem=dsend.at[i], recv_sem=drecv.at[i],
                device_id=device, device_id_type=MESH,
            )
        )
        sends[-1].start()
    attend(3)

    for slot in range(2):
        for g in range(PER_KV):
            part = acc[slot, g * TILE : (g + 1) * TILE]
            result = jnp.where(rec[slot] >= 0, part[:, HD:] / part[:, :HD], 0.0)
            ost[slot, :, g * HD : (g + 1) * HD] = result.astype(jnp.bfloat16)
    swap = pltpu.make_async_remote_copy(
        src_ref=ost.at[1 - s], dst_ref=out.at[:, mine], send_sem=osend, recv_sem=orecv,
        device_id=core, device_id_type=MESH,
    )
    swap.start()
    keep = pltpu.make_async_copy(ost.at[s], out.at[:, mine], osem)
    keep.start()

    total = devp[...]
    for i in range(7):
        sends[i].wait()
        total = total + gathered[i]
    dev[...] = jnp.where(s == 0, total[0:1], total[1:2])
    for j in range(4):
        for dy in (1, 2, 3):
            ycopy(j, dy).wait_send()
    for way in range(2):
        for piece in orders[way]:
            zcopy(way, piece).wait_send()
    keep.wait()
    swap.wait()


def whole_call(level, tab, rec, pool, fresh, q):
    caps = LEVELS[level]
    p1, p2, p3, p4 = caps
    tile = (TILE, 2 * HD)
    bf = jnp.bfloat16
    anyspace = pl.BlockSpec(memory_space=pl.ANY)
    smem = pl.BlockSpec(memory_space=pltpu.SMEM)
    vmem = pl.BlockSpec(memory_space=pltpu.VMEM)
    dma = pltpu.SemaphoreType.DMA
    return pl.pallas_call(
        functools.partial(whole_kernel, caps),
        out_shape=(
            jax.ShapeDtypeStruct((TILE, 2 * HCOLS), bf),
            jax.ShapeDtypeStruct((1, TILE), jnp.float32),
        ),
        in_specs=[smem, smem, anyspace, anyspace, anyspace],
        out_specs=(vmem, vmem),
        scratch_shapes=[
            pltpu.VMEM((2, TILE, HCOLS), bf),
            pltpu.VMEM((2,) + tile, bf),
            pltpu.VMEM((2, NT) + tile, bf),
            pltpu.VMEM((2, p1) + tile, bf),
            pltpu.VMEM((p1 + p3,) + tile, bf),
            pltpu.VMEM((2 * p2,) + tile, bf),
            pltpu.VMEM((p3 + p1,) + tile, bf),
            pltpu.VMEM((2 * p4,) + tile, bf),
            pltpu.VMEM((4, 3, 2) + tile, bf),
            pltpu.VMEM((NT, 2) + tile, bf),
            pltpu.VMEM((2, HCOLS, 2 * HD), bf),
            pltpu.VMEM((2, 2 * HD, NY * TILE), bf),
            pltpu.VMEM((2, NY * TILE, 2 * HD), bf),
            pltpu.VMEM((2, HCOLS, HD), jnp.float32),
            pltpu.VMEM((2, HCOLS, 2 * HD), jnp.float32),
            pltpu.VMEM((2, TILE, HCOLS), bf),
            pltpu.VMEM((8, TILE), jnp.float32),
            pltpu.VMEM((7, 8, TILE), jnp.float32),
            dma((2, 10)),
            dma((2, 10)),
            dma((4, 3)),
            dma((4, 3)),
            dma((3,)),
            dma((3,)),
            dma((3,)),
            dma((7,)),
            dma((7,)),
            dma,
            dma,
            dma,
        ],
        compiler_params=pltpu.CompilerParams(
            collective_id=level, has_side_effects=True, vmem_limit_bytes=52 * 2**20
        ),
    )(tab, rec, pool, fresh, q)


def on_device(cache_pool, fresh_kv, queries, stretch_owner, stretch_slot, recomp):
    entries = recomp[:, :, 0]
    live = entries >= 0
    reach = jnp.where(live, entries + 1, 0)
    tiles = jnp.stack([jnp.where(live[:, 1], NT, reach[:, 0]), reach[:, 1]], axis=1).reshape(-1)
    half = lax.rem(stretch_owner // NT, 2).reshape(-1)
    entry = ((stretch_owner // (2 * NT)) * NT + stretch_slot).reshape(-1)

    rows = jnp.arange(NZ, dtype=jnp.int32)[:, None]
    wanted = ((half[None] == rows // 4) & (tiles[None] > NY * (rows % 4))).astype(jnp.int32)
    need = jnp.max(jnp.sum(wanted[None, None] * need_weights(), axis=-1), axis=(1, 2))
    level = jnp.int32(0)
    for caps in LEVELS[:-1]:
        level = level + jnp.any(need > np.array(caps, np.int32)).astype(jnp.int32)

    smem = pl.BlockSpec(memory_space=pltpu.SMEM)
    tab = pl.pallas_call(
        tables_kernel,
        out_shape=jax.ShapeDtypeStruct((128,), jnp.int32),
        in_specs=[smem] * 3,
        out_specs=smem,
    )(tiles, half, entry)
    rec = lax.dynamic_index_in_dim(entries, lax.axis_index("req"), 0, keepdims=False)
    out, dev = lax.switch(
        level,
        [functools.partial(whole_call, i) for i in range(len(LEVELS))],
        tab, rec, cache_pool[0, 0], fresh_kv[0], queries[0],
    )
    return out[None], dev


def solution(mesh):
    placed = (
        P("seq", "req", "tp", None, None, None),
        P("req", "tp", "seq", None),
        P("req", "seq", "tp"),
        P(),
        P(),
        P(),
    )
    return jax.shard_map(
        on_device,
        mesh=mesh,
        in_specs=placed,
        out_specs=(P("req", "seq", "tp"), P("req", "seq")),
        check_vma=False,
    )
```

```python
import functools

import jax
import jax.numpy as jnp
from jax import lax
from jax.experimental import pallas as pl
from jax.experimental.pallas import tpu as pltpu
from jax.sharding import PartitionSpec as P

KVH = 8
HD = 128
TILE = 128
NT = 16
PER_KV = 12
HCOLS = PER_KV * HD
NZ = 8
NY = 4
MESH = pl.DeviceIdType.MESH
SCALE = HD**-0.5 * 1.4426950408889634
LOW = -1e30
LEVELS = ((11, 9, 6, 3), (13, 10, 7, 3), (15, 12, 9, 4), (28, 20, 12, 4))


def bits_set(word):
    shift = lax.shift_right_logical
    word = word - (shift(word, 1) & 0x55555555)
    word = (word & 0x33333333) + (shift(word, 2) & 0x33333333)
    word = (word + shift(word, 4)) & 0x0F0F0F0F
    word = word + shift(word, 8)
    return (word + shift(word, 16)) & 63


def prepare_kernel(owner, slot, recomp, tab, level, whole, column):
    me = lax.axis_index("req")
    z, y = me // NY, lax.rem(me, NY)

    def passage(r, c):
        block = owner[c, r] // NT
        side = lax.rem(block, 2)
        first, second = recomp[0, r], recomp[1, r]
        second = jnp.maximum(second + 1, 0)
        reach = second if c else jnp.where(second > 0, NT, jnp.maximum(first + 1, 0))
        return reach, side, (block // 2) * NT + slot[c, r]

    def read(row, carry):
        sets = {}
        for q in range(2 * NY):
            reach, side, e = passage(row * NY + q // 2, q % 2)
            bit = jnp.left_shift(1, e)
            low = jnp.where(side == 0, bit, 0)
            for group in range(4):
                for which, tile in ((0, NY * group), (1, NY * group + y)):
                    for k, part in ((group, low), (group + 4, bit ^ low)):
                        key = (which, k, (q // 2) % 2)
                        part = jnp.where(reach > tile, part, 0)
                        sets[key] = sets[key] | part if key in sets else part
        for (which, k, odd), word in sets.items():
            (whole, column)[which][(k * NZ + row) * 2 + odd] = word
        return carry

    lax.fori_loop(0, NZ, read, 0)

    def needs(ref, k, d, way):
        at = (k * NZ + lax.rem(k + (d if way == 0 else -d) + NZ, NZ)) * 2
        return ref[at + way] if d == 4 else ref[at] | ref[at + 1]

    def count(k, most):
        most = list(most)
        for way in range(2):
            seen = jnp.int32(0)
            for d in (4, 3, 2, 1):
                seen = seen | needs(whole, k, d, way)
                most[d - 1] = jnp.maximum(most[d - 1], bits_set(seen))
        return tuple(most)

    most = lax.fori_loop(0, NZ, count, (jnp.int32(0),) * 4)
    pick = jnp.int32(0)
    for caps in LEVELS[:-1]:
        over = functools.reduce(jnp.logical_or, [m > cap for m, cap in zip(most, caps)])
        pick = pick + jnp.where(over, 1, 0)
    level[0] = pick

    def walk(k, way, far):
        seen, groups = jnp.int32(0), []
        for d in range(4, far - 1, -1):
            wanted = needs(column, k, d, way)
            groups.append((wanted & ~seen, bits_set(seen)))
            seen = seen | wanted
        return groups

    def locate(e, groups):
        bit = jnp.left_shift(1, e)
        word, base = jnp.int32(0), jnp.int32(0)
        for new, start in groups:
            has = (new & bit) != 0
            word, base = jnp.where(has, new, word), jnp.where(has, start, base)
        return jnp.where(word != 0, base + bits_set(word & (bit - 1)), 0), word != 0

    for i in range(64):
        tab[i] = 0
    for way, sign in ((0, 1), (1, -1)):
        groups = walk(z, way, 1)
        for d, group in zip((4, 3, 2, 1), groups):
            row = lax.rem(z + sign * d + NZ, NZ)

            def send(q, carry):
                c = lax.rem(q, 2)
                r = row * NY + q // 2
                e = (owner[c, r] // (2 * NT)) * NT + slot[c, r]
                place, found = locate(e, [group])
                tab[jnp.where(found, way * 32 + place, 130)] = e
                return carry

            lax.fori_loop(0, 2 * NY, send, 0, unroll=True)
    for c in range(2):
        tab[128 + c] = recomp[c, me]
    here = [passage(me - y + q // 2, q % 2) for q in range(2 * NY)]
    for j in range(4):
        lists = []
        for way, sign in ((0, 1), (1, -1)):
            far = (j if way == 0 else 4 - j) if j else 4
            k = lax.rem(z - sign * far + NZ, NZ)
            lists.append((k // 4, walk(k, way, far)))
        for q, (reach, side, e) in enumerate(here):
            if j:
                back = side == lists[1][0]
                groups = [
                    (jnp.where(back, gb[0], gf[0]), jnp.where(back, gb[1], gf[1]))
                    for gf, gb in zip(*[pad(groups) for _, groups in lists])
                ]
                place, found = locate(e, groups)
                flag = jnp.where(back, 1, 0)
            else:
                k, groups = lists[(q // 2) % 2]
                place, found = locate(e, groups)
                flag = jnp.where(side == k, 1, 0)
                place = jnp.where(flag > 0, place, e)
            tab[64 + j * 8 + q] = place
            tab[96 + j * 8 + q] = flag


def pad(groups):
    return groups + [(jnp.int32(0), jnp.int32(0))] * (4 - len(groups))


def segments(caps):
    p1, p2, p3, p4 = caps
    head = [
        (1, 0, p4), (1, p4, p3), (2, 0, p4), (1, p3, p2), (3, 0, p4),
        (2, p4, p3), (4, 0, p4), (2, p3, p2),
    ]
    near, far = (1, p2, p1), (3, p4, p3)
    return [[piece for piece in order if piece[1] < piece[2]] for order in (head + [near, far], head + [far, near])]


def whole_kernel(
    caps, tab, pool, fresh, q, out, dev,
    qx, fx, poolbuf, stage, r1, r2, r3, r4, yst, ctx,
    qs, kt, vs, top, acc, ost, devp, gathered,
    zsend, zrecv, ysend, yrecv, xsend, xrecv, lsem, dsend, drecv, osend, orecv,
):
    s = lax.axis_index("seq")
    x = lax.axis_index("tp")
    me = lax.axis_index("req")
    z, y = me // NY, lax.rem(me, NY)
    p1, p2, p3, p4 = caps
    zdev = [(s, x, lax.rem(z + 1, NZ) * NY + y), (s, x, lax.rem(z + NZ - 1, NZ) * NY + y)]
    ydev = [(s, x, z * NY + lax.rem(y + dy, NY)) for dy in (1, 2, 3)]
    peers = [(lax.rem(s + ds, 2), lax.rem(x + dx, 4), me) for ds in range(2) for dx in range(4)][1:]
    core = peers[3]

    barrier = pltpu.get_barrier_semaphore()
    for device in peers + zdev + ydev:
        pl.semaphore_signal(barrier, inc=1, device_id=device, device_id_type=MESH)
    pl.semaphore_wait(barrier, len(peers + zdev + ydev))

    other = pl.ds(pl.multiple_of((1 - s) * HCOLS, HCOLS), HCOLS)
    mine = pl.ds(pl.multiple_of(s * HCOLS, HCOLS), HCOLS)
    swaps = [(pool.at[1 - s], poolbuf.at[s]), (q.at[:, other], qx.at[s]), (fresh.at[1 - s], fx.at[s])]
    keeps = [(pool.at[s], poolbuf.at[s]), (q.at[:, mine], qx.at[s]), (fresh.at[s], fx.at[s])]
    swaps = [
        pltpu.make_async_remote_copy(
            src_ref=src, dst_ref=dst, send_sem=xsend.at[i], recv_sem=xrecv.at[i],
            device_id=core, device_id_type=MESH,
        )
        for i, (src, dst) in enumerate(swaps)
    ]
    keeps = [pltpu.make_async_copy(src, dst, lsem.at[i]) for i, (src, dst) in enumerate(keeps)]
    for i in range(3):
        swaps[i].start()
        keeps[i].start()
    keeps[0].wait()
    swaps[0].wait()

    buffers = [
        [(stage.at[0], 0), (r1, 0), (r2, 0), (r3, 0), (r4, 0)],
        [(stage.at[1], 0), (r3, p3), (r2, p2), (r1, p1), (r4, p4)],
    ]
    orders = segments(caps)
    index = [{piece: i for i, piece in enumerate(order)} for order in orders]

    def zcopy(way, piece):
        hop, low, high = piece
        src, src_at = buffers[way][hop - 1]
        dst, dst_at = buffers[way][hop]
        i = index[way][piece]
        return pltpu.make_async_remote_copy(
            src_ref=src.at[pl.ds(src_at + low, high - low)],
            dst_ref=dst.at[pl.ds(dst_at + low, high - low)],
            send_sem=zsend.at[way, i],
            recv_sem=zrecv.at[way, i],
            device_id=zdev[way],
            device_id_type=MESH,
        )

    for step in range(len(orders[0])):
        for way in range(2):
            hop, low, high = piece = orders[way][step]
            if hop == 1:

                def fetch(place, carry):
                    row = tab[way * 32 + place]
                    stage[way, place] = poolbuf[row // NT, lax.rem(row, NT)]
                    return carry

                lax.fori_loop(low, high, fetch, 0)
            else:
                zcopy(way, (hop - 1, low, high)).wait_recv()
            zcopy(way, piece).start()
        if step == 2:
            for i in (1, 2):
                keeps[i].wait()
                swaps[i].wait()
            eye = jnp.where(
                lax.broadcasted_iota(jnp.int32, (TILE, TILE), 0)
                == lax.broadcasted_iota(jnp.int32, (TILE, TILE), 1),
                1.0,
                0.0,
            ).astype(jnp.bfloat16)
            for slot in range(2):

                def lay(g, carry):
                    rows = pl.ds(pl.multiple_of(g * TILE, TILE), TILE)
                    qs[slot, rows, :HD] = qx[slot, :, rows]
                    qs[slot, rows, HD:] = eye
                    return carry

                lax.fori_loop(0, PER_KV, lay, 0)
            vs[...] = jnp.ones(vs.shape, vs.dtype)
            top[...] = jnp.full(top.shape, LOW, top.dtype)
            acc[...] = jnp.zeros(acc.shape, acc.dtype)

    def group(j):
        return lax.rem(z - j + NZ, 4)

    def ycopy(j, dy):
        return pltpu.make_async_remote_copy(
            src_ref=yst.at[j, dy - 1],
            dst_ref=ctx.at[NY * group(j) + y],
            send_sem=ysend.at[j, dy - 1],
            recv_sem=yrecv.at[j, dy - 1],
            device_id=ydev[dy - 1],
            device_id_type=MESH,
        )

    def hand_out(j):
        for way in range(2):
            last = [(4, 0, p4), (1, p2, p1), (2, p3, p2), (3, p4, p3)]
            piece = last[j if way == 0 else (4 - j) % 4]
            if piece in index[way]:
                zcopy(way, piece).wait_recv()

        def picked(column, c):
            at = j * 8 + column * 2 + c
            place, side = tab[64 + at], tab[96 + at]
            if j:
                return (r1, r2, r3)[j - 1][place + side * caps[j - 1]]
            near = jnp.where(side > 0, 0, place)
            far = jnp.where(side > 0, place, 0)
            far = far + lax.rem(column, 2) * p4
            local = poolbuf[near // NT, lax.rem(near, NT)]
            return jnp.where(side > 0, r4[far], local)

        for dy in (2, 1, 3):
            column = lax.rem(y + dy, NY)
            for c in range(2):
                yst[j, dy - 1, c] = picked(column, c)
            ycopy(j, dy).start()
        for c in range(2):
            ctx[NY * group(j) + y, c] = picked(y, c)

    def arrived(j):
        for dy in (1, 2, 3):
            ycopy(j, dy).wait_recv()

    def attend(j):
        for c in range(2):
            entry = tab[128 + c]
            last = jnp.maximum(entry, 0) * TILE + lax.broadcasted_iota(jnp.int32, (TILE, TILE), 0)
            for i in range(NY):
                t = NY * group(j) + i
                tile = jnp.where(t == entry, fx[c], ctx[t, c])
                cols = slice(i * TILE, (i + 1) * TILE)
                kt[c, :HD, cols] = jnp.transpose(tile[:, :HD])
                vs[c, cols, HD:] = tile[:, HD:]
                at = t * TILE + lax.broadcasted_iota(jnp.int32, (TILE, TILE), 1)
                kt[c, HD:, cols] = jnp.where(at <= last, 0.0, LOW).astype(jnp.bfloat16)
        for slot in range(2):

            def block(i, carry):
                rows = pl.ds(pl.multiple_of(i * 2 * TILE, 2 * TILE), 2 * TILE)
                qq = qs[slot, rows]
                parts = [jnp.dot(qq, kt[slot], preferred_element_type=jnp.float32)]
                if slot:
                    parts.append(jnp.dot(qq[:, :HD], kt[0, :HD], preferred_element_type=jnp.float32))
                peak = functools.reduce(
                    jnp.maximum, [part[:, i * HD : (i + 1) * HD] for part in parts for i in range(NY)]
                )
                old = top[slot, rows]
                new = jnp.maximum(old, jnp.max(peak, axis=1, keepdims=True))
                top[slot, rows] = new
                wide = jnp.concatenate([new] * NY, axis=1)
                factor = jnp.exp2((old - new) * SCALE)
                total = acc[slot, rows] * jnp.concatenate([factor, factor], axis=1)
                for part, c in zip(parts, (slot, 0)):
                    weights = jnp.exp2((part - wide) * SCALE).astype(jnp.bfloat16)
                    total = total + jnp.dot(weights, vs[c], preferred_element_type=jnp.float32)
                acc[slot, rows] = total
                return carry

            lax.fori_loop(0, PER_KV // 2, block, 0, unroll=3)

    sends = [
        pltpu.make_async_remote_copy(
            src_ref=devp, dst_ref=gathered.at[i], send_sem=dsend.at[i], recv_sem=drecv.at[i],
            device_id=device, device_id_type=MESH,
        )
        for i, device in enumerate(peers)
    ]

    def turn(i, carry):
        j = lax.rem(i, 2) * 2 + i // 2

        @pl.when(i == 1)
        def _():
            hand_out(3)

        arrived(j)

        @pl.when(i == 3)
        def _():
            devp[...] = jnp.zeros(devp.shape, devp.dtype)
            for c in range(2):
                entry = tab[128 + c]
                gap = fx[c].astype(jnp.float32) - ctx[jnp.maximum(entry, 0), c].astype(jnp.float32)
                gap = gap * gap
                gap = jnp.transpose(gap[:, :HD] + gap[:, HD:])
                total = jnp.sum(gap, axis=0, keepdims=True) / (2 * KVH * HD)
                devp[c : c + 1] = jnp.where(entry >= 0, total, 0.0)
            for send in sends:
                send.start()

        attend(j)
        return carry

    hand_out(0)
    hand_out(2)
    hand_out(1)
    lax.fori_loop(0, 4, turn, 0)

    def result(slot, g):
        part = acc[slot, pl.ds(pl.multiple_of(g * TILE, TILE), TILE)]
        ratio = part[:, HD:] / part[:, :HD]
        return jnp.where(tab[128 + slot] >= 0, ratio, 0.0).astype(jnp.bfloat16)

    def put_other(g, carry):
        ost[:, pl.ds(pl.multiple_of(g * HD, HD), HD)] = result(1 - s, g)
        return carry

    def put_mine(g, carry):
        out[:, pl.ds(pl.multiple_of(s * HCOLS + g * HD, HD), HD)] = result(s, g)
        return carry

    lax.fori_loop(0, PER_KV, put_other, 0, unroll=2)
    swap = pltpu.make_async_remote_copy(
        src_ref=ost, dst_ref=out.at[:, mine], send_sem=osend, recv_sem=orecv,
        device_id=core, device_id_type=MESH,
    )
    swap.start()
    lax.fori_loop(0, PER_KV, put_mine, 0, unroll=2)

    total = devp[...]
    for i in range(7):
        sends[i].wait()
        total = total + gathered[i]
    dev[...] = jnp.where(s == 0, total[0:1], total[1:2])
    for j in range(4):
        for dy in (1, 2, 3):
            ycopy(j, dy).wait_send()
    for way in range(2):
        for piece in orders[way]:
            zcopy(way, piece).wait_send()
    swap.wait()


def whole_call(level, tab, pool, fresh, q):
    caps = LEVELS[level]
    p1, p2, p3, p4 = caps
    tile = (TILE, 2 * HD)
    bf = jnp.bfloat16
    anyspace = pl.BlockSpec(memory_space=pl.ANY)
    smem = pl.BlockSpec(memory_space=pltpu.SMEM)
    vmem = pl.BlockSpec(memory_space=pltpu.VMEM)
    dma = pltpu.SemaphoreType.DMA
    return pl.pallas_call(
        functools.partial(whole_kernel, caps),
        out_shape=(
            jax.ShapeDtypeStruct((TILE, 2 * HCOLS), bf),
            jax.ShapeDtypeStruct((1, TILE), jnp.float32),
        ),
        in_specs=[smem, anyspace, anyspace, anyspace],
        out_specs=(vmem, vmem),
        scratch_shapes=[
            pltpu.VMEM((2, TILE, HCOLS), bf),
            pltpu.VMEM((2,) + tile, bf),
            pltpu.VMEM((2, NT) + tile, bf),
            pltpu.VMEM((2, p1) + tile, bf),
            pltpu.VMEM((p1 + p3,) + tile, bf),
            pltpu.VMEM((2 * p2,) + tile, bf),
            pltpu.VMEM((p3 + p1,) + tile, bf),
            pltpu.VMEM((2 * p4,) + tile, bf),
            pltpu.VMEM((4, 3, 2) + tile, bf),
            pltpu.VMEM((NT, 2) + tile, bf),
            pltpu.VMEM((2, HCOLS, 2 * HD), bf),
            pltpu.VMEM((2, 2 * HD, NY * TILE), bf),
            pltpu.VMEM((2, NY * TILE, 2 * HD), bf),
            pltpu.VMEM((2, HCOLS, HD), jnp.float32),
            pltpu.VMEM((2, HCOLS, 2 * HD), jnp.float32),
            pltpu.VMEM((TILE, HCOLS), bf),
            pltpu.VMEM((8, TILE), jnp.float32),
            pltpu.VMEM((7, 8, TILE), jnp.float32),
            dma((2, 10)),
            dma((2, 10)),
            dma((4, 3)),
            dma((4, 3)),
            dma((3,)),
            dma((3,)),
            dma((3,)),
            dma((7,)),
            dma((7,)),
            dma,
            dma,
        ],
        compiler_params=pltpu.CompilerParams(
            collective_id=level, has_side_effects=True, vmem_limit_bytes=52 * 2**20
        ),
    )(tab, pool, fresh, q)


def on_device(cache_pool, fresh_kv, queries, stretch_owner, stretch_slot, recomp):
    smem = pl.BlockSpec(memory_space=pltpu.SMEM)
    word = jnp.int32
    tab, level = pl.pallas_call(
        prepare_kernel,
        out_shape=(jax.ShapeDtypeStruct((131,), word), jax.ShapeDtypeStruct((1,), word)),
        in_specs=[smem] * 3,
        out_specs=(smem, smem),
        scratch_shapes=[pltpu.SMEM((128,), word)] * 2,
    )(*(jnp.transpose(a.reshape(-1, 2)) for a in (stretch_owner, stretch_slot, recomp)))
    out, dev = lax.switch(
        level[0],
        [functools.partial(whole_call, i) for i in range(len(LEVELS))],
        tab, cache_pool[0, 0], fresh_kv[0], queries[0],
    )
    return out[None], dev


def solution(mesh):
    placed = (
        P("seq", "req", "tp", None, None, None),
        P("req", "tp", "seq", None),
        P("req", "seq", "tp"),
        P(),
        P(),
        P(),
    )
    return jax.shard_map(
        on_device,
        mesh=mesh,
        in_specs=placed,
        out_specs=(P("req", "seq", "tp"), P("req", "seq")),
        check_vma=False,
    )
```

```python
import functools

import jax
import jax.numpy as jnp
from jax import lax
from jax.experimental import pallas as pl
from jax.experimental.pallas import tpu as pltpu
from jax.sharding import PartitionSpec as P

KVH = 8
HD = 128
TILE = 128
NT = 16
PER_KV = 12
HCOLS = PER_KV * HD
NZ = 8
NY = 4
MESH = pl.DeviceIdType.MESH
SCALE = HD**-0.5 * 1.4426950408889634
LOW = -1e30
LEVELS = ((11, 8, 5, 3), (12, 9, 6, 3), (13, 10, 7, 4), (15, 12, 9, 4), (28, 20, 12, 4))


def bits_set(word):
    shift = lax.shift_right_logical
    word = word - (shift(word, 1) & 0x55555555)
    word = (word & 0x33333333) + (shift(word, 2) & 0x33333333)
    word = (word + shift(word, 4)) & 0x0F0F0F0F
    word = word + shift(word, 8)
    return (word + shift(word, 16)) & 63


def prepare_kernel(
    owner, slot, recomp, pool, fresh, q, tab, level, poolx, fx, qx, sets, flips, send_sem, recv_sem
):
    s = lax.axis_index("seq")
    me = lax.axis_index("req")
    z, y = me // NY, lax.rem(me, NY)
    core = (1 - s, lax.axis_index("tp"), me)
    barrier = pltpu.get_barrier_semaphore()
    pl.semaphore_signal(barrier, inc=1, device_id=core, device_id_type=MESH)
    pl.semaphore_wait(barrier, 1)
    other = pl.ds(pl.multiple_of((1 - s) * HCOLS, HCOLS), HCOLS)
    swaps = [
        pltpu.make_async_remote_copy(
            src_ref=src, dst_ref=dst, send_sem=send_sem.at[i], recv_sem=recv_sem.at[i],
            device_id=core, device_id_type=MESH,
        )
        for i, (src, dst) in enumerate(((pool.at[1 - s], poolx), (fresh.at[1 - s], fx), (q.at[:, other], qx)))
    ]
    for swap in swaps:
        swap.start()

    def passage(r, c):
        block = owner[c, r] // NT
        side = lax.rem(block, 2)
        first, second = recomp[0, r], recomp[1, r]
        second = jnp.maximum(second + 1, 0)
        reach = second if c else jnp.where(second > 0, NT, jnp.maximum(first + 1, 0))
        return reach, side, (block // 2) * NT + slot[c, r]

    def read(row, carry):
        words = {}
        for q in range(2 * NY):
            reach, side, e = passage(row * NY + q // 2, q % 2)
            bit = jnp.left_shift(1, e)
            low = jnp.where(side == 0, bit, 0)
            for group in range(4):
                wanted = reach > NY * group
                for k, part in ((group, low), (group + 4, bit ^ low)):
                    key = (k, (q // 2) % 2)
                    part = jnp.where(wanted, part, 0)
                    words[key] = words[key] | part if key in words else part
        for (k, odd), word in words.items():
            sets[(k * NZ + row) * 2 + odd] = word
        return carry

    lax.fori_loop(0, NZ, read, 0)

    def needs(k, d, way):
        at = (k * NZ + lax.rem(k + (d if way == 0 else -d) + NZ, NZ)) * 2
        return sets[at + (way ^ flips[k])] if d == 4 else sets[at] | sets[at + 1]

    def count(k, most):
        far = (k * NZ + lax.rem(k + 4, NZ)) * 2
        near = [[needs(k, d, way) for d in (3, 2, 1)] for way in range(2)]
        found, totals = [], []
        for flip in range(2):
            sizes = []
            for way in range(2):
                seen = sets[far + (way ^ flip)]
                sizes.append([bits_set(seen)])
                for more in near[way]:
                    seen = seen | more
                    sizes[way].append(bits_set(seen))
            found.append([jnp.maximum(a, b) for a, b in zip(*sizes)])
            totals.append(sum(found[flip]))
        flip = totals[1] < totals[0]
        flips[k] = jnp.where(flip, 1, 0)
        return tuple(jnp.maximum(m, jnp.where(flip, b, a)) for m, a, b in zip(most, *found))

    most = lax.fori_loop(0, NZ, count, (jnp.int32(0),) * 4)
    pick = jnp.int32(0)
    for caps in LEVELS[:-1]:
        over = functools.reduce(jnp.logical_or, [m > cap for m, cap in zip(most, caps[::-1])])
        pick = pick + jnp.where(over, 1, 0)
    level[0] = pick

    def walk(k, way, far):
        seen, groups = jnp.int32(0), []
        for d in range(4, far - 1, -1):
            wanted = needs(k, d, way)
            groups.append((wanted & ~seen, bits_set(seen)))
            seen = seen | wanted
        return groups

    def listed(place, ways):
        out = []
        for way, words in enumerate(ways):
            head = jnp.int32(0)
            for word in words[::-1]:
                head = jnp.where(word != 0, word, head)
            low = head & -head
            tab[way * 32 + place] = bits_set(low - 1) & 31
            out.append(tuple(word & ~low for word in words))
        return tuple(out)

    lax.fori_loop(
        0, LEVELS[-1][0], listed, tuple(tuple(g[0] for g in walk(z, way, 1)) for way in range(2)), unroll=2
    )
    for c in range(2):
        tab[128 + c] = recomp[c, me]
    tab[130] = flips[lax.rem(z + 4, NZ)]
    here = [passage(me - y + q // 2, q % 2) for q in range(2 * NY)]
    for j in range(4):
        lists = []
        for way, sign in ((0, 1), (1, -1)):
            far = (j if way == 0 else 4 - j) if j else 4
            k = lax.rem(z - sign * far + NZ, NZ)
            lists.append((k // 4, walk(k, way, far)))
        for q, (reach, side, e) in enumerate(here):
            back = side == lists[1][0]
            if j == 0:
                k = lax.rem(z + 4, NZ)
                groups = [(sets[(k * NZ + z) * 2 + (q // 2) % 2], jnp.int32(0))]
            else:
                groups = [
                    (jnp.where(back, gb[0], gf[0]), jnp.where(back, gb[1], gf[1]))
                    for gf, gb in zip(*[pad(groups) for _, groups in lists])
                ]
            bit = jnp.left_shift(1, e)
            word, base = jnp.int32(0), jnp.int32(0)
            for new, start in groups:
                has = (new & bit) != 0
                word, base = jnp.where(has, new, word), jnp.where(has, start, base)
            place = jnp.where(word != 0, base + bits_set(word & (bit - 1)), 0)
            if not j:
                place = jnp.where(back, place, e)
            tab[64 + j * 8 + q] = place
            tab[96 + j * 8 + q] = jnp.where(back, 1, 0)
    for swap in swaps:
        swap.wait()


def pad(groups):
    return groups + [(jnp.int32(0), jnp.int32(0))] * (4 - len(groups))


def prepare_call(owner, slot, recomp, pool, fresh, q):
    smem = pl.BlockSpec(memory_space=pltpu.SMEM)
    anyspace = pl.BlockSpec(memory_space=pl.ANY)
    word, bf = jnp.int32, jnp.bfloat16
    return pl.pallas_call(
        prepare_kernel,
        out_shape=(
            jax.ShapeDtypeStruct((131,), word),
            jax.ShapeDtypeStruct((1,), word),
            jax.ShapeDtypeStruct((NT, TILE, 2 * HD), bf),
            jax.ShapeDtypeStruct((TILE, 2 * HD), bf),
            jax.ShapeDtypeStruct((TILE, HCOLS), bf),
        ),
        in_specs=[smem] * 3 + [anyspace] * 3,
        out_specs=(smem, smem, anyspace, anyspace, anyspace),
        scratch_shapes=[
            pltpu.SMEM((128,), word),
            pltpu.SMEM((NZ,), word),
            pltpu.SemaphoreType.DMA((3,)),
            pltpu.SemaphoreType.DMA((3,)),
        ],
        compiler_params=pltpu.CompilerParams(collective_id=len(LEVELS), has_side_effects=True),
    )(owner, slot, recomp, pool, fresh, q)


def segments(caps):
    p1, p2, p3, p4 = caps
    head = [
        (1, 0, p4), (1, p4, p3), (2, 0, p4), (1, p3, p2), (3, 0, p4),
        (2, p4, p3), (4, 0, p4), (2, p3, p2),
    ]
    near, far = (1, p2, p1), (3, p4, p3)
    return [[piece for piece in order if piece[1] < piece[2]] for order in (head + [near, far], head + [far, near])]


def whole_kernel(
    caps, tab, pool, fresh, q, poolin, fin, qin, out, dev,
    qx, fx, poolbuf, stage, r1, r2, r3, r4, yst, ctx,
    qs, kt, vs, top, acc, ost, devp, gathered,
    zsend, zrecv, ysend, yrecv, lsem, dsend, drecv, osend, orecv,
):
    s = lax.axis_index("seq")
    x = lax.axis_index("tp")
    me = lax.axis_index("req")
    z, y = me // NY, lax.rem(me, NY)
    p1, p2, p3, p4 = caps
    zdev = [(s, x, lax.rem(z + 1, NZ) * NY + y), (s, x, lax.rem(z + NZ - 1, NZ) * NY + y)]
    ydev = [(s, x, z * NY + lax.rem(y + dy, NY)) for dy in (1, 2, 3)]
    peers = [(lax.rem(s + ds, 2), lax.rem(x + dx, 4), me) for ds in range(2) for dx in range(4)][1:]
    core = peers[3]

    mine = pl.ds(pl.multiple_of(s * HCOLS, HCOLS), HCOLS)
    loads = [
        pltpu.make_async_copy(src, dst, lsem.at[i])
        for i, (src, dst) in enumerate(
            (
                (pool.at[s], poolbuf.at[s]),
                (poolin, poolbuf.at[1 - s]),
                (fresh.at[s], fx.at[s]),
                (fin, fx.at[1 - s]),
                (q.at[:, mine], qx.at[s]),
                (qin, qx.at[1 - s]),
            )
        )
    ]
    for load in loads:
        load.start()
    barrier = pltpu.get_barrier_semaphore()
    for device in peers + zdev + ydev:
        pl.semaphore_signal(barrier, inc=1, device_id=device, device_id_type=MESH)
    loads[0].wait()
    loads[1].wait()
    pl.semaphore_wait(barrier, len(peers + zdev + ydev))

    buffers = [
        [(stage.at[0], 0), (r1, 0), (r2, 0), (r3, 0), (r4, 0)],
        [(stage.at[1], 0), (r3, p3), (r2, p2), (r1, p1), (r4, p4)],
    ]
    orders = segments(caps)
    index = [{piece: i for i, piece in enumerate(order)} for order in orders]

    def zcopy(way, piece):
        hop, low, high = piece
        src, src_at = buffers[way][hop - 1]
        dst, dst_at = buffers[way][hop]
        i = index[way][piece]
        return pltpu.make_async_remote_copy(
            src_ref=src.at[pl.ds(src_at + low, high - low)],
            dst_ref=dst.at[pl.ds(dst_at + low, high - low)],
            send_sem=zsend.at[way, i],
            recv_sem=zrecv.at[way, i],
            device_id=zdev[way],
            device_id_type=MESH,
        )

    for step in range(len(orders[0])):
        for way in range(2):
            hop, low, high = piece = orders[way][step]
            if hop == 1:

                def fetch(place, carry):
                    row = tab[way * 32 + place]
                    stage[way, place] = poolbuf[row // NT, lax.rem(row, NT)]
                    return carry

                lax.fori_loop(low, high, fetch, 0)
            else:
                zcopy(way, (hop - 1, low, high)).wait_recv()
            zcopy(way, piece).start()
        if step == 2:
            for load in loads[2:]:
                load.wait()
            eye = jnp.where(
                lax.broadcasted_iota(jnp.int32, (TILE, TILE), 0)
                == lax.broadcasted_iota(jnp.int32, (TILE, TILE), 1),
                1.0,
                0.0,
            ).astype(jnp.bfloat16)
            for slot in range(2):

                def lay(g, carry):
                    rows = pl.ds(pl.multiple_of(g * TILE, TILE), TILE)
                    qs[slot, rows, :HD] = qx[slot, :, rows]
                    qs[slot, rows, HD:] = eye
                    return carry

                lax.fori_loop(0, PER_KV, lay, 0)
            vs[...] = jnp.ones(vs.shape, vs.dtype)
            top[...] = jnp.full(top.shape, LOW, top.dtype)
            acc[...] = jnp.zeros(acc.shape, acc.dtype)

    def group(j):
        return lax.rem(z - j + NZ, 4)

    def ycopy(j, dy):
        return pltpu.make_async_remote_copy(
            src_ref=yst.at[j, dy - 1],
            dst_ref=ctx.at[NY * group(j) + y],
            send_sem=ysend.at[j, dy - 1],
            recv_sem=yrecv.at[j, dy - 1],
            device_id=ydev[dy - 1],
            device_id_type=MESH,
        )

    def hand_out(j):
        for way in range(2):
            last = [(4, 0, p4), (1, p2, p1), (2, p3, p2), (3, p4, p3)]
            piece = last[j if way == 0 else (4 - j) % 4]
            if piece in index[way]:
                zcopy(way, piece).wait_recv()

        def picked(column, c):
            at = j * 8 + column * 2 + c
            place, side = tab[64 + at], tab[96 + at]
            if j:
                return (r1, r2, r3)[j - 1][place + side * caps[j - 1]]
            near = jnp.where(side > 0, 0, place)
            far = jnp.where(side > 0, place, 0)
            far = far + (lax.rem(column, 2) ^ tab[130]) * p4
            local = poolbuf[near // NT, lax.rem(near, NT)]
            return jnp.where(side > 0, r4[far], local)

        for dy in (2, 1, 3):
            column = lax.rem(y + dy, NY)

            def give(c, carry):
                yst[j, dy - 1, c] = picked(column, c)
                return carry

            lax.fori_loop(0, 2, give, 0)
            ycopy(j, dy).start()

        def keep(c, carry):
            ctx[NY * group(j) + y, c] = picked(y, c)
            return carry

        lax.fori_loop(0, 2, keep, 0)

    def arrived(j):
        for dy in (1, 2, 3):
            ycopy(j, dy).wait_recv()

    def attend(j):
        for c in range(2):
            entry = tab[128 + c]
            last = jnp.maximum(entry, 0) * TILE + lax.broadcasted_iota(jnp.int32, (TILE, TILE), 0)

            def blend(i, carry):
                t = NY * group(j) + i
                tile = jnp.where(t == entry, fx[c], ctx[t, c])
                cols = pl.ds(pl.multiple_of(i * TILE, TILE), TILE)
                kt[c, :HD, cols] = jnp.transpose(tile[:, :HD])
                vs[c, cols, HD:] = tile[:, HD:]
                at = t * TILE + lax.broadcasted_iota(jnp.int32, (TILE, TILE), 1)
                kt[c, HD:, cols] = jnp.where(at <= last, 0.0, LOW).astype(jnp.bfloat16)
                return carry

            lax.fori_loop(0, NY, blend, 0, unroll=2)

    def update(slot, i):
        rows = pl.ds(pl.multiple_of(i * 2 * TILE, 2 * TILE), 2 * TILE)
        qq = qs[slot, rows]
        parts = [jnp.dot(qq, kt[slot], preferred_element_type=jnp.float32)]
        if slot:
            parts.append(jnp.dot(qq[:, :HD], kt[0, :HD], preferred_element_type=jnp.float32))
        peak = functools.reduce(
            jnp.maximum, [part[:, i * HD : (i + 1) * HD] for part in parts for i in range(NY)]
        )
        old = top[slot, rows]
        new = jnp.maximum(old, jnp.max(peak, axis=1, keepdims=True))
        top[slot, rows] = new
        wide = jnp.concatenate([new] * NY, axis=1)
        factor = jnp.exp2((old - new) * SCALE)
        total = acc[slot, rows] * jnp.concatenate([factor, factor], axis=1)
        for part, c in zip(parts, (slot, 0)):
            weights = jnp.exp2((part - wide) * SCALE).astype(jnp.bfloat16)
            total = total + jnp.dot(weights, vs[c], preferred_element_type=jnp.float32)
        acc[slot, rows] = total

    def result(slot, g):
        part = acc[slot, pl.ds(pl.multiple_of(g * TILE, TILE), TILE)]
        ratio = part[:, HD:] / part[:, :HD]
        return jnp.where(tab[128 + slot] >= 0, ratio, 0.0).astype(jnp.bfloat16)

    span = 4 * HD

    def swap(part):
        return pltpu.make_async_remote_copy(
            src_ref=ost.at[:, pl.ds(pl.multiple_of(part * span, span), span)],
            dst_ref=out.at[:, pl.ds(pl.multiple_of(s * HCOLS + part * span, span), span)],
            send_sem=osend.at[part],
            recv_sem=orecv.at[part],
            device_id=core,
            device_id_type=MESH,
        )

    sends = [
        pltpu.make_async_remote_copy(
            src_ref=devp, dst_ref=gathered.at[i], send_sem=dsend.at[i], recv_sem=drecv.at[i],
            device_id=device, device_id_type=MESH,
        )
        for i, device in enumerate(peers)
    ]

    def turn(i, carry):
        j = lax.rem(i, 2) * 2 + i // 2

        @pl.when(i == 1)
        def _():
            hand_out(3)

        arrived(j)

        @pl.when(i == 3)
        def _():
            devp[...] = jnp.zeros(devp.shape, devp.dtype)
            for c in range(2):
                entry = tab[128 + c]
                gap = fx[c].astype(jnp.float32) - ctx[jnp.maximum(entry, 0), c].astype(jnp.float32)
                gap = gap * gap
                gap = jnp.transpose(gap[:, :HD] + gap[:, HD:])
                total = jnp.sum(gap, axis=0, keepdims=True) / (2 * KVH * HD)
                devp[c : c + 1] = jnp.where(entry >= 0, total, 0.0)
            for send in sends:
                send.start()

        attend(j)

        def heads(part, carry):
            for slot in range(2):
                for n in range(2):
                    update(slot, part * 2 + n)

            @pl.when(i == 3)
            def _():
                def put(n, carry):
                    g = part * 4 + n
                    cols = pl.ds(pl.multiple_of(g * HD, HD), HD)
                    ost[:, cols] = result(1 - s, g)
                    out[:, pl.ds(pl.multiple_of(s * HCOLS + g * HD, HD), HD)] = result(s, g)
                    return carry

                lax.fori_loop(0, 4, put, 0)
                swap(part).start()

            return carry

        lax.fori_loop(0, PER_KV // 4, heads, 0)
        return carry

    hand_out(0)
    hand_out(2)
    hand_out(1)
    lax.fori_loop(0, 4, turn, 0)

    total = devp[...]
    for i in range(7):
        sends[i].wait()
        total = total + gathered[i]
    dev[...] = jnp.where(s == 0, total[0:1], total[1:2])
    for j in range(4):
        for dy in (1, 2, 3):
            ycopy(j, dy).wait_send()
    for way in range(2):
        for piece in orders[way]:
            zcopy(way, piece).wait_send()
    for part in range(PER_KV // 4):
        swap(part).wait()


def whole_call(level, *args):
    caps = LEVELS[level]
    p1, p2, p3, p4 = caps
    tile = (TILE, 2 * HD)
    bf = jnp.bfloat16
    anyspace = pl.BlockSpec(memory_space=pl.ANY)
    smem = pl.BlockSpec(memory_space=pltpu.SMEM)
    vmem = pl.BlockSpec(memory_space=pltpu.VMEM)
    dma = pltpu.SemaphoreType.DMA
    return pl.pallas_call(
        functools.partial(whole_kernel, caps),
        out_shape=(
            jax.ShapeDtypeStruct((TILE, 2 * HCOLS), bf),
            jax.ShapeDtypeStruct((1, TILE), jnp.float32),
        ),
        in_specs=[smem] + [anyspace] * 6,
        out_specs=(vmem, vmem),
        scratch_shapes=[
            pltpu.VMEM((2, TILE, HCOLS), bf),
            pltpu.VMEM((2,) + tile, bf),
            pltpu.VMEM((2, NT) + tile, bf),
            pltpu.VMEM((2, p1) + tile, bf),
            pltpu.VMEM((p1 + p3,) + tile, bf),
            pltpu.VMEM((2 * p2,) + tile, bf),
            pltpu.VMEM((p3 + p1,) + tile, bf),
            pltpu.VMEM((2 * p4,) + tile, bf),
            pltpu.VMEM((4, 3, 2) + tile, bf),
            pltpu.VMEM((NT, 2) + tile, bf),
            pltpu.VMEM((2, HCOLS, 2 * HD), bf),
            pltpu.VMEM((2, 2 * HD, NY * TILE), bf),
            pltpu.VMEM((2, NY * TILE, 2 * HD), bf),
            pltpu.VMEM((2, HCOLS, HD), jnp.float32),
            pltpu.VMEM((2, HCOLS, 2 * HD), jnp.float32),
            pltpu.VMEM((TILE, HCOLS), bf),
            pltpu.VMEM((8, TILE), jnp.float32),
            pltpu.VMEM((7, 8, TILE), jnp.float32),
            dma((2, 10)),
            dma((2, 10)),
            dma((4, 3)),
            dma((4, 3)),
            dma((6,)),
            dma((7,)),
            dma((7,)),
            dma((3,)),
            dma((3,)),
        ],
        compiler_params=pltpu.CompilerParams(
            collective_id=level, has_side_effects=True, vmem_limit_bytes=52 * 2**20
        ),
    )(*args)


def on_device(cache_pool, fresh_kv, queries, stretch_owner, stretch_slot, recomp):
    pool, fresh, q = cache_pool[0, 0], fresh_kv[0], queries[0]
    small = [jnp.transpose(a.reshape(-1, 2)) for a in (stretch_owner, stretch_slot, recomp)]
    tab, level, *swapped = prepare_call(*small, pool, fresh, q)
    out, dev = lax.switch(
        level[0],
        [functools.partial(whole_call, i) for i in range(len(LEVELS))],
        tab, pool, fresh, q, *swapped,
    )
    return out[None], dev


def solution(mesh):
    placed = (
        P("seq", "req", "tp", None, None, None),
        P("req", "tp", "seq", None),
        P("req", "seq", "tp"),
        P(),
        P(),
        P(),
    )
    return jax.shard_map(
        on_device,
        mesh=mesh,
        in_specs=placed,
        out_specs=(P("req", "seq", "tp"), P("req", "seq")),
        check_vma=False,
    )
```

```python
import functools

import jax
import jax.numpy as jnp
from jax import lax
from jax.experimental import pallas as pl
from jax.experimental.pallas import tpu as pltpu
from jax.sharding import PartitionSpec as P

KVH = 8
HD = 128
TILE = 128
NT = 16
PER_KV = 12
HCOLS = PER_KV * HD
NZ = 8
NY = 4
MESH = pl.DeviceIdType.MESH
SCALE = HD**-0.5 * 1.4426950408889634
LOW = -1e30
LEVELS = ((11, 8, 5, 3), (12, 9, 6, 3), (13, 10, 7, 4), (15, 12, 9, 4), (28, 20, 12, 4))


def bits_set(word):
    shift = lax.shift_right_logical
    word = word - (shift(word, 1) & 0x55555555)
    word = (word & 0x33333333) + (shift(word, 2) & 0x33333333)
    word = (word + shift(word, 4)) & 0x0F0F0F0F
    word = word + shift(word, 8)
    return (word + shift(word, 16)) & 63


def prepare_kernel(
    owner, slot, recomp, pool, fresh, q, tab, level, poolx, fx, qx, sets, flips, send_sem, recv_sem
):
    s = lax.axis_index("seq")
    me = lax.axis_index("req")
    z, y = me // NY, lax.rem(me, NY)
    core = (1 - s, lax.axis_index("tp"), me)
    barrier = pltpu.get_barrier_semaphore()
    pl.semaphore_signal(barrier, inc=1, device_id=core, device_id_type=MESH)
    pl.semaphore_wait(barrier, 1)
    other = pl.ds(pl.multiple_of((1 - s) * HCOLS, HCOLS), HCOLS)
    swaps = [
        pltpu.make_async_remote_copy(
            src_ref=src, dst_ref=dst, send_sem=send_sem.at[i], recv_sem=recv_sem.at[i],
            device_id=core, device_id_type=MESH,
        )
        for i, (src, dst) in enumerate(((pool.at[1 - s], poolx), (fresh.at[1 - s], fx), (q.at[:, other], qx)))
    ]
    for swap in swaps:
        swap.start()

    def passage(r, c):
        block = owner[c, r] // NT
        side = lax.rem(block, 2)
        first, second = recomp[0, r], recomp[1, r]
        second = jnp.maximum(second + 1, 0)
        reach = second if c else jnp.where(second > 0, NT, jnp.maximum(first + 1, 0))
        return reach, side, (block // 2) * NT + slot[c, r]

    def read(row, carry):
        words = {}
        for q in range(2 * NY):
            reach, side, e = passage(row * NY + q // 2, q % 2)
            bit = jnp.left_shift(1, e)
            low = jnp.where(side == 0, bit, 0)
            for group in range(4):
                wanted = reach > NY * group
                for k, part in ((group, low), (group + 4, bit ^ low)):
                    key = (k, (q // 2) % 2)
                    part = jnp.where(wanted, part, 0)
                    words[key] = words[key] | part if key in words else part
        for (k, odd), word in words.items():
            sets[(k * NZ + row) * 2 + odd] = word
        return carry

    lax.fori_loop(0, NZ, read, 0)

    def needs(k, d, way):
        at = (k * NZ + lax.rem(k + (d if way == 0 else -d) + NZ, NZ)) * 2
        return sets[at + (way ^ flips[k])] if d == 4 else sets[at] | sets[at + 1]

    def count(k, most):
        far = (k * NZ + lax.rem(k + 4, NZ)) * 2
        near = [[needs(k, d, way) for d in (3, 2, 1)] for way in range(2)]
        found, totals = [], []
        for flip in range(2):
            sizes = []
            for way in range(2):
                seen = sets[far + (way ^ flip)]
                sizes.append([bits_set(seen)])
                for more in near[way]:
                    seen = seen | more
                    sizes[way].append(bits_set(seen))
            found.append([jnp.maximum(a, b) for a, b in zip(*sizes)])
            totals.append(sum(found[flip]))
        flip = totals[1] < totals[0]
        flips[k] = jnp.where(flip, 1, 0)
        return tuple(jnp.maximum(m, jnp.where(flip, b, a)) for m, a, b in zip(most, *found))

    most = lax.fori_loop(0, NZ, count, (jnp.int32(0),) * 4)
    pick = jnp.int32(0)
    for caps in LEVELS[:-1]:
        over = functools.reduce(jnp.logical_or, [m > cap for m, cap in zip(most, caps[::-1])])
        pick = pick + jnp.where(over, 1, 0)
    level[0] = pick

    def walk(k, way, far):
        seen, groups = jnp.int32(0), []
        for d in range(4, far - 1, -1):
            wanted = needs(k, d, way)
            groups.append((wanted & ~seen, bits_set(seen)))
            seen = seen | wanted
        return groups

    def listed(place, ways):
        out = []
        for way, words in enumerate(ways):
            head = jnp.int32(0)
            for word in words[::-1]:
                head = jnp.where(word != 0, word, head)
            low = head & -head
            tab[way * 32 + place] = bits_set(low - 1) & 31
            out.append(tuple(word & ~low for word in words))
        return tuple(out)

    lax.fori_loop(
        0, LEVELS[-1][0], listed, tuple(tuple(g[0] for g in walk(z, way, 1)) for way in range(2)), unroll=2
    )
    for c in range(2):
        tab[128 + c] = recomp[c, me]
    tab[130] = flips[lax.rem(z + 4, NZ)]
    here = [passage(me - y + q // 2, q % 2) for q in range(2 * NY)]
    for j in range(4):
        lists = []
        for way, sign in ((0, 1), (1, -1)):
            far = (j if way == 0 else 4 - j) if j else 4
            k = lax.rem(z - sign * far + NZ, NZ)
            lists.append((k // 4, walk(k, way, far)))
        for q, (reach, side, e) in enumerate(here):
            back = side == lists[1][0]
            if j == 0:
                k = lax.rem(z + 4, NZ)
                groups = [(sets[(k * NZ + z) * 2 + (q // 2) % 2], jnp.int32(0))]
            else:
                groups = [
                    (jnp.where(back, gb[0], gf[0]), jnp.where(back, gb[1], gf[1]))
                    for gf, gb in zip(*[pad(groups) for _, groups in lists])
                ]
            bit = jnp.left_shift(1, e)
            word, base = jnp.int32(0), jnp.int32(0)
            for new, start in groups:
                has = (new & bit) != 0
                word, base = jnp.where(has, new, word), jnp.where(has, start, base)
            place = jnp.where(word != 0, base + bits_set(word & (bit - 1)), 0)
            if not j:
                place = jnp.where(back, place, e)
            tab[64 + j * 8 + q] = place
            tab[96 + j * 8 + q] = jnp.where(back, 1, 0)
    for swap in swaps:
        swap.wait()


def pad(groups):
    return groups + [(jnp.int32(0), jnp.int32(0))] * (4 - len(groups))


def prepare_call(owner, slot, recomp, pool, fresh, q):
    smem = pl.BlockSpec(memory_space=pltpu.SMEM)
    anyspace = pl.BlockSpec(memory_space=pl.ANY)
    word, bf = jnp.int32, jnp.bfloat16
    return pl.pallas_call(
        prepare_kernel,
        out_shape=(
            jax.ShapeDtypeStruct((131,), word),
            jax.ShapeDtypeStruct((1,), word),
            jax.ShapeDtypeStruct((NT, TILE, 2 * HD), bf),
            jax.ShapeDtypeStruct((TILE, 2 * HD), bf),
            jax.ShapeDtypeStruct((TILE, HCOLS), bf),
        ),
        in_specs=[smem] * 3 + [anyspace] * 3,
        out_specs=(smem, smem, anyspace, anyspace, anyspace),
        scratch_shapes=[
            pltpu.SMEM((128,), word),
            pltpu.SMEM((NZ,), word),
            pltpu.SemaphoreType.DMA((3,)),
            pltpu.SemaphoreType.DMA((3,)),
        ],
        compiler_params=pltpu.CompilerParams(collective_id=len(LEVELS), has_side_effects=True),
    )(owner, slot, recomp, pool, fresh, q)


def segments(caps):
    p1, p2, p3, p4 = caps
    head = [(hop, low, high) for hop in (1, 2) for low, high in ((0, p4), (p4, p3), (p3, p2))]
    near, far, last = [(1, p2, p1)], [(3, 0, p4), (3, p4, p3)], [(4, 0, p4)]
    return [
        [piece for piece in order if piece[1] < piece[2]]
        for order in (head + near + far + last, head + far + near + last)
    ]


def whole_kernel(
    caps, tab, pool, fresh, q, poolin, fin, qin, out, dev,
    qx, fx, poolbuf, stage, r1, r2, r3, r4, yst, ctx,
    qs, kt, vs, top, acc, ost, devp, gathered,
    zsend, zrecv, ysend, yrecv, lsem, dsend, drecv, osend, orecv,
):
    s = lax.axis_index("seq")
    x = lax.axis_index("tp")
    me = lax.axis_index("req")
    z, y = me // NY, lax.rem(me, NY)
    p1, p2, p3, p4 = caps
    zdev = [(s, x, lax.rem(z + 1, NZ) * NY + y), (s, x, lax.rem(z + NZ - 1, NZ) * NY + y)]
    ydev = [(s, x, z * NY + lax.rem(y + dy, NY)) for dy in (1, 2, 3)]
    peers = [(lax.rem(s + ds, 2), lax.rem(x + dx, 4), me) for ds in range(2) for dx in range(4)][1:]
    core = peers[3]

    mine = pl.ds(pl.multiple_of(s * HCOLS, HCOLS), HCOLS)
    loads = [
        pltpu.make_async_copy(src, dst, lsem.at[i])
        for i, (src, dst) in enumerate(
            (
                (pool.at[s], poolbuf.at[s]),
                (poolin, poolbuf.at[1 - s]),
                (fresh.at[s], fx.at[s]),
                (fin, fx.at[1 - s]),
                (q.at[:, mine], qx.at[s]),
                (qin, qx.at[1 - s]),
            )
        )
    ]
    for load in loads:
        load.start()
    barrier = pltpu.get_barrier_semaphore()
    for device in peers + zdev + ydev:
        pl.semaphore_signal(barrier, inc=1, device_id=device, device_id_type=MESH)
    loads[0].wait()
    loads[1].wait()
    pl.semaphore_wait(barrier, len(peers + zdev + ydev))

    buffers = [
        [(stage.at[0], 0), (r1, 0), (r2, 0), (r3, 0), (r4, 0)],
        [(stage.at[1], 0), (r3, p3), (r2, p2), (r1, p1), (r4, p4)],
    ]
    orders = segments(caps)
    index = [{piece: i for i, piece in enumerate(order)} for order in orders]

    def zcopy(way, piece):
        hop, low, high = piece
        src, src_at = buffers[way][hop - 1]
        dst, dst_at = buffers[way][hop]
        i = index[way][piece]
        return pltpu.make_async_remote_copy(
            src_ref=src.at[pl.ds(src_at + low, high - low)],
            dst_ref=dst.at[pl.ds(dst_at + low, high - low)],
            send_sem=zsend.at[way, i],
            recv_sem=zrecv.at[way, i],
            device_id=zdev[way],
            device_id_type=MESH,
        )

    def issue(way, step):
        hop, low, high = piece = orders[way][step]
        if hop == 1:

            def fetch(place, carry):
                row = tab[way * 32 + place]
                stage[way, place] = poolbuf[row // NT, lax.rem(row, NT)]
                return carry

            lax.fori_loop(low, high, fetch, 0)
        else:
            zcopy(way, (hop - 1, low, high)).wait_recv()
        zcopy(way, piece).start()

    for step in range(len(orders[0]) - 1):
        for way in range(2):
            issue(way, step)
        if step == 2:
            for load in loads[2:]:
                load.wait()
            eye = jnp.where(
                lax.broadcasted_iota(jnp.int32, (TILE, TILE), 0)
                == lax.broadcasted_iota(jnp.int32, (TILE, TILE), 1),
                1.0,
                0.0,
            ).astype(jnp.bfloat16)
            for slot in range(2):

                def lay(g, carry):
                    rows = pl.ds(pl.multiple_of(g * TILE, TILE), TILE)
                    qs[slot, rows, :HD] = qx[slot, :, rows]
                    qs[slot, rows, HD:] = eye
                    top[slot, rows] = jnp.full((TILE, HD), LOW, top.dtype)
                    acc[slot, rows] = jnp.zeros((TILE, 2 * HD), acc.dtype)
                    return carry

                lax.fori_loop(0, PER_KV, lay, 0)

            def fill(i, carry):
                rows = pl.ds(pl.multiple_of(i * TILE, TILE), TILE)
                for c in range(2):
                    vs[c, rows, :HD] = jnp.ones((TILE, HD), vs.dtype)
                return carry

            lax.fori_loop(0, NY, fill, 0)

    def group(j):
        return lax.rem(z - j + NZ, 4)

    def ycopy(j, dy):
        return pltpu.make_async_remote_copy(
            src_ref=yst.at[j, dy - 1],
            dst_ref=ctx.at[NY * group(j) + y],
            send_sem=ysend.at[j, dy - 1],
            recv_sem=yrecv.at[j, dy - 1],
            device_id=ydev[dy - 1],
            device_id_type=MESH,
        )

    def hand_out(j):
        for way in range(2):
            last = [(4, 0, p4), (1, p2, p1), (2, p3, p2), (3, p4, p3)]
            piece = last[j if way == 0 else (4 - j) % 4]
            if piece in index[way]:
                zcopy(way, piece).wait_recv()

        def picked(column, c):
            at = j * 8 + column * 2 + c
            place, side = tab[64 + at], tab[96 + at]
            if j:
                return (r1, r2, r3)[j - 1][place + side * caps[j - 1]]
            near = jnp.where(side > 0, 0, place)
            far = jnp.where(side > 0, place, 0)
            far = far + (lax.rem(column, 2) ^ tab[130]) * p4
            local = poolbuf[near // NT, lax.rem(near, NT)]
            return jnp.where(side > 0, r4[far], local)

        for dy in (2, 1, 3):
            column = lax.rem(y + dy, NY)

            def give(c, carry):
                yst[j, dy - 1, c] = picked(column, c)
                return carry

            lax.fori_loop(0, 2, give, 0)
            ycopy(j, dy).start()

        def keep(c, carry):
            ctx[NY * group(j) + y, c] = picked(y, c)
            return carry

        lax.fori_loop(0, 2, keep, 0)

    def arrived(j):
        for dy in (1, 2, 3):
            ycopy(j, dy).wait_recv()

    def attend(j):
        for c in range(2):
            entry = tab[128 + c]
            last = jnp.maximum(entry, 0) * TILE + lax.broadcasted_iota(jnp.int32, (TILE, TILE), 0)

            def blend(i, carry):
                t = NY * group(j) + i
                tile = jnp.where(t == entry, fx[c], ctx[t, c])
                cols = pl.ds(pl.multiple_of(i * TILE, TILE), TILE)
                kt[c, :HD, cols] = jnp.transpose(tile[:, :HD])
                vs[c, cols, HD:] = tile[:, HD:]
                at = t * TILE + lax.broadcasted_iota(jnp.int32, (TILE, TILE), 1)
                kt[c, HD:, cols] = jnp.where(at <= last, 0.0, LOW).astype(jnp.bfloat16)
                return carry

            lax.fori_loop(0, NY, blend, 0, unroll=2)

    def update(slot, i):
        rows = pl.ds(pl.multiple_of(i * 2 * TILE, 2 * TILE), 2 * TILE)
        qq = qs[slot, rows]
        parts = [jnp.dot(qq, kt[slot], preferred_element_type=jnp.float32)]
        if slot:
            parts.append(jnp.dot(qq[:, :HD], kt[0, :HD], preferred_element_type=jnp.float32))
        peak = functools.reduce(
            jnp.maximum, [part[:, i * HD : (i + 1) * HD] for part in parts for i in range(NY)]
        )
        old = top[slot, rows]
        new = jnp.maximum(old, jnp.max(peak, axis=1, keepdims=True))
        top[slot, rows] = new
        wide = jnp.concatenate([new] * NY, axis=1)
        factor = jnp.exp2((old - new) * SCALE)
        total = acc[slot, rows] * jnp.concatenate([factor, factor], axis=1)
        for part, c in zip(parts, (slot, 0)):
            weights = jnp.exp2((part - wide) * SCALE).astype(jnp.bfloat16)
            total = total + jnp.dot(weights, vs[c], preferred_element_type=jnp.float32)
        acc[slot, rows] = total

    def result(slot, g):
        part = acc[slot, pl.ds(pl.multiple_of(g * TILE, TILE), TILE)]
        ratio = part[:, HD:] / part[:, :HD]
        return jnp.where(tab[128 + slot] >= 0, ratio, 0.0).astype(jnp.bfloat16)

    span = 6 * HD

    def swap(part):
        return pltpu.make_async_remote_copy(
            src_ref=ost.at[:, pl.ds(pl.multiple_of(part * span, span), span)],
            dst_ref=out.at[:, pl.ds(pl.multiple_of(s * HCOLS + part * span, span), span)],
            send_sem=osend.at[part],
            recv_sem=orecv.at[part],
            device_id=core,
            device_id_type=MESH,
        )

    sends = [
        pltpu.make_async_remote_copy(
            src_ref=devp, dst_ref=gathered.at[i], send_sem=dsend.at[i], recv_sem=drecv.at[i],
            device_id=device, device_id_type=MESH,
        )
        for i, device in enumerate(peers)
    ]

    def turn(unit, carry):
        i, part = unit // 2, lax.rem(unit, 2)
        j = 2 - i + 3 * (i // 2) - 2 * (i // 3)

        @pl.when(unit == 0)
        def _():
            issue(1, -1)
            hand_out(1)

        @pl.when(unit == 1)
        def _():
            issue(0, -1)

        @pl.when(unit == 2)
        def _():
            hand_out(3)

        @pl.when(unit == 3)
        def _():
            hand_out(0)

        @pl.when(part == 0)
        def _():
            arrived(j)
            attend(j)

        @pl.when(unit == 6)
        def _():
            devp[...] = jnp.zeros(devp.shape, devp.dtype)
            for c in range(2):
                entry = tab[128 + c]
                gap = fx[c].astype(jnp.float32) - ctx[jnp.maximum(entry, 0), c].astype(jnp.float32)
                gap = gap * gap
                gap = jnp.transpose(gap[:, :HD] + gap[:, HD:])
                total = jnp.sum(gap, axis=0, keepdims=True) / (2 * KVH * HD)
                devp[c : c + 1] = jnp.where(entry >= 0, total, 0.0)
            for send in sends:
                send.start()

        for slot in range(2):
            for n in range(3):
                update(slot, part * 3 + n)

        @pl.when(i == 3)
        def _():
            def put(n, carry):
                g = part * 6 + n
                cols = pl.ds(pl.multiple_of(g * HD, HD), HD)
                ost[:, cols] = result(1 - s, g)
                out[:, pl.ds(pl.multiple_of(s * HCOLS + g * HD, HD), HD)] = result(s, g)
                return carry

            lax.fori_loop(0, 6, put, 0)
            swap(part).start()

        return carry

    hand_out(2)
    lax.fori_loop(0, 8, turn, 0)

    total = devp[...]
    for i in range(7):
        sends[i].wait()
        total = total + gathered[i]
    dev[...] = jnp.where(s == 0, total[0:1], total[1:2])
    for j in range(4):
        for dy in (1, 2, 3):
            ycopy(j, dy).wait_send()
    for way in range(2):
        for piece in orders[way]:
            zcopy(way, piece).wait_send()
    for part in range(2):
        swap(part).wait()


def whole_call(level, *args):
    caps = LEVELS[level]
    p1, p2, p3, p4 = caps
    tile = (TILE, 2 * HD)
    bf = jnp.bfloat16
    anyspace = pl.BlockSpec(memory_space=pl.ANY)
    smem = pl.BlockSpec(memory_space=pltpu.SMEM)
    vmem = pl.BlockSpec(memory_space=pltpu.VMEM)
    dma = pltpu.SemaphoreType.DMA
    return pl.pallas_call(
        functools.partial(whole_kernel, caps),
        out_shape=(
            jax.ShapeDtypeStruct((TILE, 2 * HCOLS), bf),
            jax.ShapeDtypeStruct((1, TILE), jnp.float32),
        ),
        in_specs=[smem] + [anyspace] * 6,
        out_specs=(vmem, vmem),
        scratch_shapes=[
            pltpu.VMEM((2, TILE, HCOLS), bf),
            pltpu.VMEM((2,) + tile, bf),
            pltpu.VMEM((2, NT) + tile, bf),
            pltpu.VMEM((2, p1) + tile, bf),
            pltpu.VMEM((p1 + p3,) + tile, bf),
            pltpu.VMEM((2 * p2,) + tile, bf),
            pltpu.VMEM((p3 + p1,) + tile, bf),
            pltpu.VMEM((2 * p4,) + tile, bf),
            pltpu.VMEM((4, 3, 2) + tile, bf),
            pltpu.VMEM((NT, 2) + tile, bf),
            pltpu.VMEM((2, HCOLS, 2 * HD), bf),
            pltpu.VMEM((2, 2 * HD, NY * TILE), bf),
            pltpu.VMEM((2, NY * TILE, 2 * HD), bf),
            pltpu.VMEM((2, HCOLS, HD), jnp.float32),
            pltpu.VMEM((2, HCOLS, 2 * HD), jnp.float32),
            pltpu.VMEM((TILE, HCOLS), bf),
            pltpu.VMEM((8, TILE), jnp.float32),
            pltpu.VMEM((7, 8, TILE), jnp.float32),
            dma((2, 10)),
            dma((2, 10)),
            dma((4, 3)),
            dma((4, 3)),
            dma((6,)),
            dma((7,)),
            dma((7,)),
            dma((3,)),
            dma((3,)),
        ],
        compiler_params=pltpu.CompilerParams(
            collective_id=level, has_side_effects=True, vmem_limit_bytes=52 * 2**20
        ),
    )(*args)


def on_device(cache_pool, fresh_kv, queries, stretch_owner, stretch_slot, recomp):
    pool, fresh, q = cache_pool[0, 0], fresh_kv[0], queries[0]
    small = [jnp.transpose(a.reshape(-1, 2)) for a in (stretch_owner, stretch_slot, recomp)]
    tab, level, *swapped = prepare_call(*small, pool, fresh, q)
    out, dev = lax.switch(
        level[0],
        [functools.partial(whole_call, i) for i in range(len(LEVELS))],
        tab, pool, fresh, q, *swapped,
    )
    return out[None], dev


def solution(mesh):
    placed = (
        P("seq", "req", "tp", None, None, None),
        P("req", "tp", "seq", None),
        P("req", "seq", "tp"),
        P(),
        P(),
        P(),
    )
    return jax.shard_map(
        on_device,
        mesh=mesh,
        in_specs=placed,
        out_specs=(P("req", "seq", "tp"), P("req", "seq")),
        check_vma=False,
    )
```

```python
import functools

import jax
import jax.numpy as jnp
from jax import lax
from jax.experimental import pallas as pl
from jax.experimental.pallas import tpu as pltpu
from jax.sharding import PartitionSpec as P

KVH = 8
HD = 128
TILE = 128
NT = 16
PER_KV = 12
HCOLS = PER_KV * HD
NZ = 8
NY = 4
MESH = pl.DeviceIdType.MESH
SCALE = HD**-0.5 * 1.4426950408889634
LOW = -1e30
LEVELS = ((11, 8, 5, 3), (12, 9, 6, 3), (13, 10, 7, 4), (15, 12, 9, 4), (28, 20, 12, 4))


def bits_set(word):
    shift = lax.shift_right_logical
    word = word - (shift(word, 1) & 0x55555555)
    word = (word & 0x33333333) + (shift(word, 2) & 0x33333333)
    word = (word + shift(word, 4)) & 0x0F0F0F0F
    word = word + shift(word, 8)
    return (word + shift(word, 16)) & 63


SETS, FLIPS, OWN, HERE = 64, 192, 200, 202


def prepare_kernel(
    owner, slot, recomp, pool, tab, level, poolx, send_sem, recv_sem
):
    s = lax.axis_index("seq")
    me = lax.axis_index("req")
    z, y = me // NY, lax.rem(me, NY)
    core = (1 - s, lax.axis_index("tp"), me)
    barrier = pltpu.get_barrier_semaphore()
    pl.semaphore_signal(barrier, inc=1, device_id=core, device_id_type=MESH)
    pl.semaphore_wait(barrier, 1)
    swap = pltpu.make_async_remote_copy(
        src_ref=pool.at[1 - s], dst_ref=poolx, send_sem=send_sem, recv_sem=recv_sem,
        device_id=core, device_id_type=MESH,
    )
    swap.start()

    def passage(r, c):
        block = owner[c, r] // NT
        side = lax.rem(block, 2)
        first, second = recomp[0, r], recomp[1, r]
        second = jnp.maximum(second + 1, 0)
        reach = second if c else jnp.where(second > 0, NT, jnp.maximum(first + 1, 0))
        return reach, side, (block // 2) * NT + slot[c, r]

    def read(row, carry):
        words = {}
        for q in range(2 * NY):
            reach, side, e = passage(row * NY + q // 2, q % 2)
            bit = jnp.left_shift(1, e)
            low = jnp.where(side == 0, bit, 0)
            for group in range(4):
                wanted = reach > NY * group
                for k, part in ((group, low), (group + 4, bit ^ low)):
                    key = (k, (q // 2) % 2)
                    part = jnp.where(wanted, part, 0)
                    words[key] = words[key] | part if key in words else part
        for (k, odd), word in words.items():
            tab[SETS + (k * NZ + row) * 2 + odd] = word
        return carry

    lax.fori_loop(0, NZ, read, 0)

    def count(k, most):
        far = SETS + (k * NZ + lax.rem(k + 4, NZ)) * 2
        near = [[needs(tab, k, d, way) for d in (3, 2, 1)] for way in range(2)]
        found, totals = [], []
        for flip in range(2):
            sizes = []
            for way in range(2):
                seen = tab[far + (way ^ flip)]
                sizes.append([bits_set(seen)])
                for more in near[way]:
                    seen = seen | more
                    sizes[way].append(bits_set(seen))
            found.append([jnp.maximum(a, b) for a, b in zip(*sizes)])
            totals.append(sum(found[flip]))
        flip = totals[1] < totals[0]
        tab[FLIPS + k] = jnp.where(flip, 1, 0)
        return tuple(jnp.maximum(m, jnp.where(flip, b, a)) for m, a, b in zip(most, *found))

    most = lax.fori_loop(0, NZ, count, (jnp.int32(0),) * 4)
    pick = jnp.int32(0)
    for caps in LEVELS[:-1]:
        over = functools.reduce(jnp.logical_or, [m > cap for m, cap in zip(most, caps[::-1])])
        pick = pick + jnp.where(over, 1, 0)
    level[0] = pick

    def listed(place, ways):
        out = []
        for way, words in enumerate(ways):
            head = jnp.int32(0)
            for word in words[::-1]:
                head = jnp.where(word != 0, word, head)
            low = head & -head
            tab[way * 32 + place] = bits_set(low - 1) & 31
            out.append(tuple(word & ~low for word in words))
        return tuple(out)

    lax.fori_loop(
        0, LEVELS[-1][0], listed, tuple(tuple(g[0] for g in walk(tab, z, way, 1)) for way in range(2)), unroll=2
    )
    for c in range(2):
        tab[OWN + c] = recomp[c, me]
    for q in range(2 * NY):
        _, side, e = passage(me - y + q // 2, q % 2)
        tab[HERE + q] = e
        tab[HERE + 8 + q] = side
    swap.wait()


def needs(tab, k, d, way):
    at = SETS + (k * NZ + lax.rem(k + (d if way == 0 else -d) + NZ, NZ)) * 2
    return tab[at + (way ^ tab[FLIPS + k])] if d == 4 else tab[at] | tab[at + 1]


def walk(tab, k, way, far):
    seen, groups = jnp.int32(0), []
    for d in range(4, far - 1, -1):
        wanted = needs(tab, k, d, way)
        groups.append((wanted & ~seen, bits_set(seen)))
        seen = seen | wanted
    return groups


def pad(groups):
    return groups + [(jnp.int32(0), jnp.int32(0))] * (4 - len(groups))


def find_places(z, tab, picks):
    for j in range(4):
        lists = []
        for way, sign in ((0, 1), (1, -1)):
            far = (j if way == 0 else 4 - j) if j else 4
            k = lax.rem(z - sign * far + NZ, NZ)
            lists.append((k // 4, k, walk(tab, k, way, far)))

        def find(q, carry):
            e, side = tab[HERE + q], tab[HERE + 8 + q]
            back = side == lists[1][0]
            if j == 0:
                groups = [(tab[SETS + (lists[1][1] * NZ + z) * 2 + lax.rem(q // 2, 2)], jnp.int32(0))]
            else:
                groups = [
                    (jnp.where(back, gb[0], gf[0]), jnp.where(back, gb[1], gf[1]))
                    for gf, gb in zip(*[pad(groups) for _, _, groups in lists])
                ]
            bit = jnp.left_shift(1, e)
            word, base = jnp.int32(0), jnp.int32(0)
            for new, start in groups:
                has = (new & bit) != 0
                word, base = jnp.where(has, new, word), jnp.where(has, start, base)
            place = jnp.where(word != 0, base + bits_set(word & (bit - 1)), 0)
            if j == 0:
                place = jnp.where(back, place, e)
            picks[j * 8 + q] = place
            picks[32 + j * 8 + q] = jnp.where(back, 1, 0)
            return carry

        lax.fori_loop(0, 2 * NY, find, 0)


def prepare_call(owner, slot, recomp, pool):
    smem = pl.BlockSpec(memory_space=pltpu.SMEM)
    anyspace = pl.BlockSpec(memory_space=pl.ANY)
    word, bf = jnp.int32, jnp.bfloat16
    return pl.pallas_call(
        prepare_kernel,
        out_shape=(
            jax.ShapeDtypeStruct((256,), word),
            jax.ShapeDtypeStruct((1,), word),
            jax.ShapeDtypeStruct((NT, TILE, 2 * HD), bf),
        ),
        in_specs=[smem] * 3 + [anyspace],
        out_specs=(smem, smem, anyspace),
        scratch_shapes=[pltpu.SemaphoreType.DMA, pltpu.SemaphoreType.DMA],
        compiler_params=pltpu.CompilerParams(collective_id=len(LEVELS), has_side_effects=True),
    )(owner, slot, recomp, pool)


def segments(caps):
    p1, p2, p3, p4 = caps
    head = [(hop, low, high) for hop in (1, 2) for low, high in ((0, p4), (p4, p3), (p3, p2))]
    near, far, last = [(1, p2, p1)], [(3, 0, p4), (3, p4, p3)], [(4, 0, p4)]
    return [
        [piece for piece in order if piece[1] < piece[2]]
        for order in (head + near + far + last, head + far + near + last)
    ]


def whole_kernel(
    caps, tab, pool, fresh, q, poolin, out, dev, picks,
    qx, fx, poolbuf, stage, r1, r2, r3, r4, yst, ctx,
    qs, kt, vs, top, acc, ost, devp, gathered,
    zsend, zrecv, ysend, yrecv, xsend, xrecv, lsem, dsend, drecv, osend, orecv,
):
    s = lax.axis_index("seq")
    x = lax.axis_index("tp")
    me = lax.axis_index("req")
    z, y = me // NY, lax.rem(me, NY)
    p1, p2, p3, p4 = caps
    zdev = [(s, x, lax.rem(z + 1, NZ) * NY + y), (s, x, lax.rem(z + NZ - 1, NZ) * NY + y)]
    ydev = [(s, x, z * NY + lax.rem(y + dy, NY)) for dy in (1, 2, 3)]
    peers = [(lax.rem(s + ds, 2), lax.rem(x + dx, 4), me) for ds in range(2) for dx in range(4)][1:]
    core = peers[3]

    mine = pl.ds(pl.multiple_of(s * HCOLS, HCOLS), HCOLS)
    loads = [
        pltpu.make_async_copy(src, dst, lsem.at[i])
        for i, (src, dst) in enumerate(
            (
                (pool.at[s], poolbuf.at[s]),
                (poolin, poolbuf.at[1 - s]),
                (fresh.at[s], fx.at[s]),
                (q.at[:, mine], qx.at[s]),
            )
        )
    ]
    for load in loads:
        load.start()
    barrier = pltpu.get_barrier_semaphore()
    for device in peers + zdev + ydev:
        pl.semaphore_signal(barrier, inc=1, device_id=device, device_id_type=MESH)
    loads[0].wait()
    loads[1].wait()
    pl.semaphore_wait(barrier, len(peers + zdev + ydev))
    other = pl.ds(pl.multiple_of((1 - s) * HCOLS, HCOLS), HCOLS)
    swaps = [
        pltpu.make_async_remote_copy(
            src_ref=src, dst_ref=dst, send_sem=xsend.at[i], recv_sem=xrecv.at[i],
            device_id=core, device_id_type=MESH,
        )
        for i, (src, dst) in enumerate(((fresh.at[1 - s], fx.at[s]), (q.at[:, other], qx.at[s])))
    ]

    buffers = [
        [(stage.at[0], 0), (r1, 0), (r2, 0), (r3, 0), (r4, 0)],
        [(stage.at[1], 0), (r3, p3), (r2, p2), (r1, p1), (r4, p4)],
    ]
    orders = segments(caps)
    index = [{piece: i for i, piece in enumerate(order)} for order in orders]

    def zcopy(way, piece):
        hop, low, high = piece
        src, src_at = buffers[way][hop - 1]
        dst, dst_at = buffers[way][hop]
        i = index[way][piece]
        return pltpu.make_async_remote_copy(
            src_ref=src.at[pl.ds(src_at + low, high - low)],
            dst_ref=dst.at[pl.ds(dst_at + low, high - low)],
            send_sem=zsend.at[way, i],
            recv_sem=zrecv.at[way, i],
            device_id=zdev[way],
            device_id_type=MESH,
        )

    def issue(way, step):
        hop, low, high = piece = orders[way][step]
        if hop == 1:

            def fetch(place, carry):
                row = tab[way * 32 + place]
                stage[way, place] = poolbuf[row // NT, lax.rem(row, NT)]
                return carry

            lax.fori_loop(low, high, fetch, 0)
        else:
            zcopy(way, (hop - 1, low, high)).wait_recv()
        zcopy(way, piece).start()

    for step in range(len(orders[0]) - 1):
        for way in range(2):
            issue(way, step)
        if step == 2:
            for trade in swaps:
                trade.start()
            find_places(z, tab, picks)
            for load in loads[2:]:
                load.wait()
            for trade in swaps:
                trade.wait()
            eye = jnp.where(
                lax.broadcasted_iota(jnp.int32, (TILE, TILE), 0)
                == lax.broadcasted_iota(jnp.int32, (TILE, TILE), 1),
                1.0,
                0.0,
            ).astype(jnp.bfloat16)
            for slot in range(2):

                def lay(g, carry):
                    rows = pl.ds(pl.multiple_of(g * TILE, TILE), TILE)
                    qs[slot, rows, :HD] = qx[slot, :, rows]
                    qs[slot, rows, HD:] = eye
                    top[slot, rows] = jnp.full((TILE, HD), LOW, top.dtype)
                    acc[slot, rows] = jnp.zeros((TILE, 2 * HD), acc.dtype)
                    return carry

                lax.fori_loop(0, PER_KV, lay, 0)

            def fill(i, carry):
                rows = pl.ds(pl.multiple_of(i * TILE, TILE), TILE)
                for c in range(2):
                    vs[c, rows, :HD] = jnp.ones((TILE, HD), vs.dtype)
                return carry

            lax.fori_loop(0, NY, fill, 0)

    def group(j):
        return lax.rem(z - j + NZ, 4)

    def ycopy(j, dy):
        return pltpu.make_async_remote_copy(
            src_ref=yst.at[j, dy - 1],
            dst_ref=ctx.at[NY * group(j) + y],
            send_sem=ysend.at[j, dy - 1],
            recv_sem=yrecv.at[j, dy - 1],
            device_id=ydev[dy - 1],
            device_id_type=MESH,
        )

    def hand_out(j):
        for way in range(2):
            last = [(4, 0, p4), (1, p2, p1), (2, p3, p2), (3, p4, p3)]
            piece = last[j if way == 0 else (4 - j) % 4]
            if piece in index[way]:
                zcopy(way, piece).wait_recv()

        def picked(column, c):
            at = j * 8 + column * 2 + c
            place, side = picks[at], picks[32 + at]
            if j:
                return (r1, r2, r3)[j - 1][place + side * caps[j - 1]]
            near = jnp.where(side > 0, 0, place)
            far = jnp.where(side > 0, place, 0)
            far = far + (lax.rem(column, 2) ^ tab[FLIPS + lax.rem(z + 4, NZ)]) * p4
            local = poolbuf[near // NT, lax.rem(near, NT)]
            return jnp.where(side > 0, r4[far], local)

        for dy in (2, 1, 3):
            column = lax.rem(y + dy, NY)

            def give(c, carry):
                yst[j, dy - 1, c] = picked(column, c)
                return carry

            lax.fori_loop(0, 2, give, 0)
            ycopy(j, dy).start()

        def keep(c, carry):
            ctx[NY * group(j) + y, c] = picked(y, c)
            return carry

        lax.fori_loop(0, 2, keep, 0)

    def arrived(j):
        for dy in (1, 2, 3):
            ycopy(j, dy).wait_recv()

    def attend(j):
        for c in range(2):
            entry = tab[OWN + c]
            last = jnp.maximum(entry, 0) * TILE + lax.broadcasted_iota(jnp.int32, (TILE, TILE), 0)

            def blend(i, carry):
                t = NY * group(j) + i
                tile = jnp.where(t == entry, fx[c], ctx[t, c])
                cols = pl.ds(pl.multiple_of(i * TILE, TILE), TILE)
                kt[c, :HD, cols] = jnp.transpose(tile[:, :HD])
                vs[c, cols, HD:] = tile[:, HD:]
                at = t * TILE + lax.broadcasted_iota(jnp.int32, (TILE, TILE), 1)
                kt[c, HD:, cols] = jnp.where(at <= last, 0.0, LOW).astype(jnp.bfloat16)
                return carry

            lax.fori_loop(0, NY, blend, 0, unroll=2)

    def update(slot, i):
        rows = pl.ds(pl.multiple_of(i * 2 * TILE, 2 * TILE), 2 * TILE)
        qq = qs[slot, rows]
        parts = [jnp.dot(qq, kt[slot], preferred_element_type=jnp.float32)]
        if slot:
            parts.append(jnp.dot(qq[:, :HD], kt[0, :HD], preferred_element_type=jnp.float32))
        peak = functools.reduce(
            jnp.maximum, [part[:, i * HD : (i + 1) * HD] for part in parts for i in range(NY)]
        )
        old = top[slot, rows]
        new = jnp.maximum(old, jnp.max(peak, axis=1, keepdims=True))
        top[slot, rows] = new
        wide = jnp.concatenate([new] * NY, axis=1)
        factor = jnp.exp2((old - new) * SCALE)
        total = acc[slot, rows] * jnp.concatenate([factor, factor], axis=1)
        for part, c in zip(parts, (slot, 0)):
            weights = jnp.exp2((part - wide) * SCALE).astype(jnp.bfloat16)
            total = total + jnp.dot(weights, vs[c], preferred_element_type=jnp.float32)
        acc[slot, rows] = total

    def result(slot, g):
        part = acc[slot, pl.ds(pl.multiple_of(g * TILE, TILE), TILE)]
        ratio = part[:, HD:] / part[:, :HD]
        return jnp.where(tab[OWN + slot] >= 0, ratio, 0.0).astype(jnp.bfloat16)

    span = 6 * HD

    def swap(part):
        return pltpu.make_async_remote_copy(
            src_ref=ost.at[:, pl.ds(pl.multiple_of(part * span, span), span)],
            dst_ref=out.at[:, pl.ds(pl.multiple_of(s * HCOLS + part * span, span), span)],
            send_sem=osend.at[part],
            recv_sem=orecv.at[part],
            device_id=core,
            device_id_type=MESH,
        )

    sends = [
        pltpu.make_async_remote_copy(
            src_ref=devp, dst_ref=gathered.at[i], send_sem=dsend.at[i], recv_sem=drecv.at[i],
            device_id=device, device_id_type=MESH,
        )
        for i, device in enumerate(peers)
    ]

    def turn(unit, carry):
        i, part = unit // 2, lax.rem(unit, 2)
        j = 2 - i + 3 * (i // 2) - 2 * (i // 3)

        @pl.when(unit == 0)
        def _():
            issue(1, -1)
            hand_out(1)

        @pl.when(unit == 1)
        def _():
            issue(0, -1)

        @pl.when(unit == 2)
        def _():
            hand_out(3)

        @pl.when(unit == 3)
        def _():
            hand_out(0)

        @pl.when(part == 0)
        def _():
            arrived(j)
            attend(j)

        @pl.when(unit == 6)
        def _():
            devp[...] = jnp.zeros(devp.shape, devp.dtype)
            for c in range(2):
                entry = tab[OWN + c]
                gap = fx[c].astype(jnp.float32) - ctx[jnp.maximum(entry, 0), c].astype(jnp.float32)
                gap = gap * gap
                gap = jnp.transpose(gap[:, :HD] + gap[:, HD:])
                total = jnp.sum(gap, axis=0, keepdims=True) / (2 * KVH * HD)
                devp[c : c + 1] = jnp.where(entry >= 0, total, 0.0)
            for send in sends:
                send.start()

        for slot in range(2):
            for n in range(3):
                update(slot, part * 3 + n)

        @pl.when(i == 3)
        def _():
            def put(n, carry):
                g = part * 6 + n
                cols = pl.ds(pl.multiple_of(g * HD, HD), HD)
                ost[:, cols] = result(1 - s, g)
                out[:, pl.ds(pl.multiple_of(s * HCOLS + g * HD, HD), HD)] = result(s, g)
                return carry

            lax.fori_loop(0, 6, put, 0)
            swap(part).start()

        return carry

    hand_out(2)
    lax.fori_loop(0, 8, turn, 0)

    total = devp[...]
    for i in range(7):
        sends[i].wait()
        total = total + gathered[i]
    dev[...] = jnp.where(s == 0, total[0:1], total[1:2])
    for j in range(4):
        for dy in (1, 2, 3):
            ycopy(j, dy).wait_send()
    for way in range(2):
        for piece in orders[way]:
            zcopy(way, piece).wait_send()
    for part in range(2):
        swap(part).wait()


def whole_call(level, *args):
    caps = LEVELS[level]
    p1, p2, p3, p4 = caps
    tile = (TILE, 2 * HD)
    bf = jnp.bfloat16
    anyspace = pl.BlockSpec(memory_space=pl.ANY)
    smem = pl.BlockSpec(memory_space=pltpu.SMEM)
    vmem = pl.BlockSpec(memory_space=pltpu.VMEM)
    dma = pltpu.SemaphoreType.DMA
    return pl.pallas_call(
        functools.partial(whole_kernel, caps),
        out_shape=(
            jax.ShapeDtypeStruct((TILE, 2 * HCOLS), bf),
            jax.ShapeDtypeStruct((1, TILE), jnp.float32),
        ),
        in_specs=[smem] + [anyspace] * 4,
        out_specs=(vmem, vmem),
        scratch_shapes=[
            pltpu.SMEM((64,), jnp.int32),
            pltpu.VMEM((2, TILE, HCOLS), bf),
            pltpu.VMEM((2,) + tile, bf),
            pltpu.VMEM((2, NT) + tile, bf),
            pltpu.VMEM((2, p1) + tile, bf),
            pltpu.VMEM((p1 + p3,) + tile, bf),
            pltpu.VMEM((2 * p2,) + tile, bf),
            pltpu.VMEM((p3 + p1,) + tile, bf),
            pltpu.VMEM((2 * p4,) + tile, bf),
            pltpu.VMEM((4, 3, 2) + tile, bf),
            pltpu.VMEM((NT, 2) + tile, bf),
            pltpu.VMEM((2, HCOLS, 2 * HD), bf),
            pltpu.VMEM((2, 2 * HD, NY * TILE), bf),
            pltpu.VMEM((2, NY * TILE, 2 * HD), bf),
            pltpu.VMEM((2, HCOLS, HD), jnp.float32),
            pltpu.VMEM((2, HCOLS, 2 * HD), jnp.float32),
            pltpu.VMEM((TILE, HCOLS), bf),
            pltpu.VMEM((8, TILE), jnp.float32),
            pltpu.VMEM((7, 8, TILE), jnp.float32),
            dma((2, 10)),
            dma((2, 10)),
            dma((4, 3)),
            dma((4, 3)),
            dma((2,)),
            dma((2,)),
            dma((4,)),
            dma((7,)),
            dma((7,)),
            dma((3,)),
            dma((3,)),
        ],
        compiler_params=pltpu.CompilerParams(
            collective_id=level, has_side_effects=True, vmem_limit_bytes=52 * 2**20
        ),
    )(*args)


def on_device(cache_pool, fresh_kv, queries, stretch_owner, stretch_slot, recomp):
    pool, fresh, q = cache_pool[0, 0], fresh_kv[0], queries[0]
    small = [jnp.transpose(a.reshape(-1, 2)) for a in (stretch_owner, stretch_slot, recomp)]
    tab, level, swapped = prepare_call(*small, pool)
    out, dev = lax.switch(
        level[0],
        [functools.partial(whole_call, i) for i in range(len(LEVELS))],
        tab, pool, fresh, q, swapped,
    )
    return out[None], dev


def solution(mesh):
    placed = (
        P("seq", "req", "tp", None, None, None),
        P("req", "tp", "seq", None),
        P("req", "seq", "tp"),
        P(),
        P(),
        P(),
    )
    return jax.shard_map(
        on_device,
        mesh=mesh,
        in_specs=placed,
        out_specs=(P("req", "seq", "tp"), P("req", "seq")),
        check_vma=False,
    )
```
